256 devices in a mesh: dp: 32 (over x, z_hi, core), comp: 8 (over y, z_lo).
Axes of the slice: x: 4, y: 4, z: 8 (z_hi: 4, z_lo: 2; z = z_hi * 2 + z_lo), core: 2. Of those that a mesh axis runs over, the one named last changes fastest.
Arguments:
- points: bfloat16 [131072, 128], P('dp'), may hold values from -13 to 13
- means: bfloat16 [16384, 128], P(('dp', 'comp')), may hold values from -0.59375 to 0.59375
- variances: float32 [16384], P(('dp', 'comp')), may hold values from 0.5 to 2
- log_weights: float32 [16384], P(('dp', 'comp')), may hold values from -11.5 to -8
Outputs:
- new_means: bfloat16 [16384, 128], P(('dp', 'comp'))
- new_variances: float32 [16384], P(('dp', 'comp'))
- new_log_weights: float32 [16384], P(('dp', 'comp'))
- point_loglik: float32 [131072], P('dp')
The draws below stay inside these ranges and needn't reach their ends.
All inputs are finite; a program needn't handle non-finite values.
Results may differ from the reference program's by a relative error of at most 0.0023.
Values may be sent and summed in bfloat16 or wider, within the bound.
A program may use at most 64 MiB of HBM per device.

```python
import math
import jax
import jax.numpy as jnp
from jax import lax

D = 128
K = 16384
NPTS = 131072


def mixture_centres(key):
    return jnp.clip(0.15 * jax.random.normal(key, (K, D), jnp.float32), -0.59375, 0.59375)


def draw_means(key, part):
    return mixture_centres(key).astype(jnp.bfloat16)


def draw_points(key, part):
    centres = mixture_centres(key)
    key = jax.random.fold_in(key, 7)
    key_pick, key_noise, key_scale = jax.random.split(key, 3)
    chosen = jax.random.randint(key_pick, (NPTS,), 0, K)
    noise = jnp.clip(jax.random.normal(key_noise, (NPTS, D), jnp.float32), -4.0, 4.0)
    scale = jnp.exp(jax.random.uniform(key_scale, (NPTS, 1), jnp.float32, jnp.log(0.5), jnp.log(2.5)))
    return (centres[chosen] + scale * noise).astype(jnp.bfloat16)


def level_of(own_key, extent, shards, least, top_value):
    def one(position, parts):
        steps = jax.random.uniform(jax.random.fold_in(jax.random.fold_in(own_key, 6), position), (parts,), jnp.float32, least / len(shards), top_value / len(shards))
        return jnp.repeat(jnp.exp(steps), extent[position] // parts).reshape((-1,) + (1,) * (len(extent) - position - 1))

    factor_of = one(*shards[0])
    for cut in shards[1:]:
        factor_of = factor_of * one(*cut)
    return factor_of


def setup_inputs(seed: int = 0) -> dict:
    seeds = jax.random.split(jax.random.key(seed), 5)
    return {
        "points": draw_points(jax.random.fold_in(seeds[4], 71), 0),
        "means": draw_means(jax.random.fold_in(seeds[4], 71), 0),
        "variances": jnp.clip(jnp.exp(math.log(2.0) - 1.3862944 * jax.random.uniform(seeds[2], (K,), jnp.float32) ** level_of(seeds[2], (K,), ((0, 256),), -0.2, 0.2)), 0.5, 2.0),
        "log_weights": jnp.clip(-11.5 + 3.5 * jax.random.uniform(seeds[3], (K,), jnp.float32) ** level_of(seeds[3], (K,), ((0, 256),), -0.2, 0.2), -11.5, -8.0),
    }


two_pi = 6.283185307179586
prior_strength = 1.0


def log_density(block, block_sq, centres, centre_sq, half_inverse, offset):
    cross = lax.dot_general(block, centres, (((1,), (1,)), ((), ())), preferred_element_type=jnp.float32)
    return offset[None, :] - (block_sq[:, None] + centre_sq[None, :] - 2.0 * cross) * half_inverse[None, :]


def update_step(sums, counts, squares, prior_means, prior_var, total_points, components):
    width = sums.shape[1]
    denom = counts + prior_strength
    centre = (sums + prior_strength * prior_means) / denom[:, None]
    spread = (squares - 2.0 * jnp.sum(centre * sums, axis=1) + counts * jnp.sum(centre * centre, axis=1)
              + prior_strength * width * prior_var) / (width * denom)
    weight = jnp.log((counts + prior_strength) / (total_points + components * prior_strength))
    return centre.astype(jnp.bfloat16), spread, weight


def reference(points, means, variances, log_weights):
    centre_f = means.astype(jnp.float32)
    centre_sq = jnp.sum(centre_f * centre_f, axis=1)
    half_inverse = 0.5 / variances
    offset = log_weights - 0.5 * D * jnp.log(two_pi * variances)
    npoints = points.shape[0]
    block_rows = math.gcd(npoints, 1024)
    block_count = npoints // block_rows
    blocks = points.reshape(block_count, block_rows, D)
    block_sq = jnp.sum(blocks.astype(jnp.float32) ** 2, axis=2)

    def visit(carry, item):
        sums, counts, squares = carry
        block, bsq = item
        logd = log_density(block, bsq, means, centre_sq, half_inverse, offset)
        peak = jnp.max(logd, axis=1)
        mass = jnp.sum(jnp.exp(logd - peak[:, None]), axis=1)
        loglik = peak + jnp.log(mass)
        prob = jnp.exp(logd - loglik[:, None])
        counts = counts + jnp.sum(prob, axis=0)
        squares = squares + jnp.dot(bsq, prob, precision=lax.Precision.HIGHEST)
        sums = sums + lax.dot_general(prob, block.astype(jnp.float32), (((0,), (0,)), ((), ())),
                                      precision=lax.Precision.HIGHEST, preferred_element_type=jnp.float32)
        return (sums, counts, squares), loglik

    start = (jnp.zeros((K, D), jnp.float32), jnp.zeros((K,), jnp.float32), jnp.zeros((K,), jnp.float32))
    (sums, counts, squares), loglik = lax.scan(visit, start, (blocks, block_sq))
    new_means, new_var, new_logw = update_step(sums, counts, squares, centre_f, variances, npoints, K)
    return new_means, new_var, new_logw, loglik.reshape(npoints)
```

```python
import functools

import jax
import jax.numpy as jnp
from jax import lax
from jax.experimental import pallas as pl
from jax.experimental.pallas import tpu as pltpu
from jax.sharding import PartitionSpec as P

MESH = pl.DeviceIdType.MESH
F32 = jnp.float32
BF16 = jnp.bfloat16

COMPONENTS = 16384
LOG2E = 1.4426950408889634
LN2 = 0.6931471805599453
TWO_PI = 6.283185307179586

XS, ZS, CORES = 4, 4, 2
WIDTH = 128
OWN = 64
BLOCK = 80
CHUNK = 512
TILE = 512

BASE = {
    (0, 0): 0, (1, 0): 4,
    (0, 1): 8, (0, 3): 12,
    (1, 1): 16, (1, 3): 20,
    (0, 2): 24, (1, 2): 28,
}
SIB = {0: 0, 1: 4, 3: 8, 2: 12}


def split3(v):
    hi = v.astype(BF16).astype(F32)
    mid = (v - hi).astype(BF16).astype(F32)
    lo = (v - hi - mid).astype(BF16).astype(F32)
    return hi, mid, lo


def rows16(parts, lanes):
    row = lax.broadcasted_iota(jnp.int32, (16, lanes), 0)
    out = jnp.zeros((16, lanes), F32)
    for i, part in parts.items():
        out = jnp.where(row == i, jnp.broadcast_to(part, (16, lanes)), out)
    return out


def spread_rows(tile, table):
    return lax.dot_general(tile, table, (((0,), (0,)), ((), ())), preferred_element_type=F32)


def body(
    comps, npoints, total_points,
    points, means, var, logw,
    out_means, out_var, out_logw, out_lik,
    blocks, centres, scale, pts_t, pts, prob, peak, mass, lse, sums, sib,
    x_out, x_in, z_out, z_in,
    g_send, g_recv, l_send, l_recv, r_send, r_recv,
):
    dp = lax.axis_index("dp")
    cp = lax.axis_index("comp")
    core = dp % CORES
    zh = (dp // CORES) % ZS
    xx = dp // (CORES * ZS)

    def dp_at(dx, dz, dc):
        return (
            ((xx + dx) % XS) * (ZS * CORES)
            + ((zh + dz) % ZS) * CORES
            + (core + dc) % CORES
        )

    z_peer = {d: {"dp": dp_at(0, d, 0)} for d in (1, 2, 3)}
    x_peer = {d: {"dp": dp_at(d, 0, 0)} for d in (1, 2, 3)}
    sibling = {"dp": dp_at(0, 0, 1)}
    c_peer = {d: {"comp": (cp + d) % comps} for d in range(1, comps)}

    barrier = pltpu.get_barrier_semaphore()
    everyone = [*z_peer.values(), *x_peer.values(), sibling, *c_peer.values()]
    for peer in everyone:
        pl.semaphore_signal(barrier, inc=1, device_id=peer, device_id_type=MESH)

    m = means[...]
    mf = m.astype(F32)
    msq = mf * mf
    msq_hi = msq.astype(BF16)
    msq_lo = (msq - msq_hi.astype(F32)).astype(BF16)
    ones = jnp.ones((16, WIDTH), BF16)
    nt = (((1,), (1,)), ((), ()))
    centre_sq = (
        lax.dot_general(ones, msq_hi, nt, preferred_element_type=F32)
        + lax.dot_general(ones, msq_lo, nt, preferred_element_type=F32)
    )[0:1, :]
    v = var[...]
    offset = logw[...] - 0.5 * WIDTH * jnp.log(TWO_PI * v)
    e_hi, e_mid, e_lo = split3(v * offset - 0.5 * centre_sq)
    a_hi, a_mid, a_lo = split3(LOG2E / v)
    blocks[0, 0:OWN, :] = m
    blocks[0, OWN:BLOCK, :] = jnp.zeros((16, WIDTH), BF16)
    blocks[0, OWN:BLOCK, 0:OWN] = rows16(
        {0: e_hi, 1: e_mid, 2: e_lo, 3: a_hi, 4: a_mid, 5: a_lo, 6: jnp.ones_like(v)}, OWN
    ).astype(BF16)

    pl.semaphore_wait(barrier, len(everyone))

    sends = []

    def remote(src, dst, send, recv, peer):
        copy = pltpu.make_async_remote_copy(
            src_ref=src, dst_ref=dst, send_sem=send, recv_sem=recv,
            device_id=peer, device_id_type=MESH,
        )
        copy.start()
        sends.append(copy)

    counter = [0]

    def gather_send(src, dst, n, peer):
        i = counter[0]
        counter[0] += 1
        remote(
            blocks.at[pl.ds(src, n)], blocks.at[pl.ds(dst, n)],
            g_send.at[i], g_recv.at[dst], peer,
        )

    def gather_wait(slot, n):
        pltpu.make_async_copy(
            blocks.at[pl.ds(slot, n)], blocks.at[pl.ds(slot, n)], g_recv.at[slot]
        ).wait()

    for d in (2, 1, 3):
        gather_send(0, BASE[0, 0] + ZS - d, 1, z_peer[d])
    gather_send(0, BASE[1, 0], 1, sibling)
    for d in (2, 1, 3):
        gather_send(0, BASE[0, XS - d], 1, x_peer[d])

    pts_t[WIDTH + 16 : 2 * WIDTH, :] = jnp.zeros((WIDTH - 16, npoints), BF16)
    row16 = lax.broadcasted_iota(jnp.int32, (16, WIDTH), 0)
    col16 = lax.broadcasted_iota(jnp.int32, (16, WIDTH), 1)
    eye16 = jnp.where(row16 == col16, 1.0, 0.0).astype(BF16)

    def prepare(j, carry):
        for u in range(4):
            at = pl.ds(pl.multiple_of((j * 4 + u) * WIDTH, WIDTH), WIDTH)
            x = points[at, :]
            xt = x.astype(F32).T
            half = -0.5 * jnp.sum(xt * xt, axis=0, keepdims=True)
            b_hi, b_mid, b_lo = split3(half)
            one = jnp.ones_like(half)
            tile = rows16({0: one, 1: one, 2: one, 3: b_hi, 4: b_mid, 5: b_lo}, WIDTH).astype(BF16)
            pts_t[0:WIDTH, at] = xt.astype(BF16)
            pts_t[WIDTH : WIDTH + 16, at] = tile
            pts[at, 0:WIDTH] = x
            pts[at, WIDTH : 2 * WIDTH] = lax.dot_general(
                tile, eye16, (((0,), (0,)), ((), ())), preferred_element_type=F32
            ).astype(BF16)
        return carry

    lax.fori_loop(0, npoints // WIDTH // 4, prepare, 0)

    for dz in (1, 3, 2):
        gather_wait(BASE[0, 0] + dz, 1)
        for d in (2, 1, 3):
            gather_send(dz, BASE[0, XS - d] + dz, 1, x_peer[d])
        gather_send(dz, BASE[1, 0] + dz, 1, sibling)

    row = lax.broadcasted_iota(jnp.int32, (16, 2 * WIDTH), 0)
    col = lax.broadcasted_iota(jnp.int32, (16, 2 * WIDTH), 1)
    put = ((row < 3) & (col == row)) | ((row == 6) & (col >= 3) & (col < 6))
    put = put | ((row >= 3) & (row < 6) & (col >= WIDTH))
    table = jnp.where(put, 1.0, 0.0).astype(BF16)

    def expand(first, n):
        for s in range(first, first + n):
            at = slice(s * OWN, (s + 1) * OWN)
            wide = spread_rows(blocks[s, OWN:BLOCK, :], table)[0:OWN, :]
            centres[at, 0:WIDTH] = blocks[s, 0:OWN, :]
            centres[at, WIDTH : 2 * WIDTH] = wide[:, 0:WIDTH].astype(BF16)
            scale[at, :] = wide[:, WIDTH : 2 * WIDTH]

    def first_pass(c):
        at = slice(c * CHUNK, (c + 1) * CHUNK)

        def half(h, carry):
            for t in range(npoints // TILE // 2):
                ns = pl.ds(pl.multiple_of(h * (npoints // 2) + t * TILE, TILE), TILE)
                y = jnp.dot(centres[at, :], pts_t[:, ns], preferred_element_type=F32)
                y = y * jnp.concatenate([scale[at, :]] * (TILE // WIDTH), axis=1)
                top = jnp.max(y, axis=0, keepdims=True)
                p = jnp.exp2(y - top)
                prob[at, ns] = p
                peak[c : c + 1, ns] = top
                mass[c : c + 1, ns] = jnp.sum(p, axis=0, keepdims=True)
            return carry

        lax.fori_loop(0, 2, half, 0)

    for dz in range(ZS):
        gather_wait(BASE[1, 0] + dz, 1)
    expand(0, 8)
    first_pass(0)
    for dx in (1, 3):
        for dz in range(ZS):
            gather_wait(BASE[0, dx] + dz, 1)
        gather_send(BASE[0, dx], BASE[1, dx], ZS, sibling)
    expand(8, 8)
    first_pass(1)
    for dz in range(ZS):
        gather_wait(BASE[0, 2] + dz, 1)
    gather_send(BASE[0, 2], BASE[1, 2], ZS, sibling)
    for dx in (1, 3):
        gather_wait(BASE[1, dx], ZS)
    expand(16, 8)
    first_pass(2)
    gather_wait(BASE[1, 2], ZS)
    expand(24, 8)
    first_pass(3)

    chunks = 4
    top = jnp.max(peak[0:chunks, :], axis=0, keepdims=True)
    total = jnp.sum(mass[0:chunks, :] * jnp.exp2(peak[0:chunks, :] - top), axis=0, keepdims=True)
    lse[0] = top + jnp.log(total) * LOG2E
    for d in range(1, comps):
        remote(lse.at[0], lse.at[comps - d], l_send.at[d], l_recv.at[comps - d], c_peer[d])
    for d in range(1, comps):
        pltpu.make_async_copy(lse.at[d], lse.at[d], l_recv.at[d]).wait()
    top = lse[0]
    for d in range(1, comps):
        top = jnp.maximum(top, lse[d])
    total = jnp.exp2(lse[0] - top)
    for d in range(1, comps):
        total = total + jnp.exp2(lse[d] - top)
    lik = top + jnp.log(total) * LOG2E
    out_lik[...] = lik * LN2
    for c in range(chunks):
        peak[c : c + 1, :] = jnp.exp2(peak[c : c + 1, :] - lik)

    def second_pass(c):
        at = slice(c * CHUNK, (c + 1) * CHUNK)
        acc = jnp.zeros((CHUNK, 2 * WIDTH), F32)
        for t in range(npoints // 1024):
            ns = slice(t * 1024, (t + 1) * 1024)
            p = (prob[at, ns] * peak[c : c + 1, ns]).astype(BF16)
            acc = acc + jnp.dot(p, pts[ns, :], preferred_element_type=F32)
        sums[at, :] = acc

    def span(first, n):
        return pl.ds(first * OWN, n * OWN)

    def to_sibling(i, dx, n):
        remote(
            sums.at[span(BASE[1, dx], n)], sib.at[span(SIB[dx], n)],
            r_send.at[i], r_recv.at[i], sibling,
        )

    def from_sibling(i, dx, n):
        ref = sib.at[span(SIB[dx], n)]
        pltpu.make_async_copy(ref, ref, r_recv.at[i]).wait()

    def stats_of(extra):
        t = extra.T
        return t[0:1, :], t[3:4, :] + t[4:5, :] + t[5:6, :]

    def pack_stats(cnt, sq):
        c_hi, c_mid, c_lo = split3(cnt)
        s_hi, s_mid, s_lo = split3(sq)
        parts = {0: c_hi, 1: c_mid, 2: c_lo, 3: s_hi, 4: s_mid, 5: s_lo}
        return rows16(parts, cnt.shape[1]).astype(BF16)

    def chip_sum(dx):
        a = slice(BASE[0, dx] * OWN, (BASE[0, dx] + ZS) * OWN)
        b = slice(SIB[dx] * OWN, (SIB[dx] + ZS) * OWN)
        return sums[a, :] + sib[b, :]

    span4 = ZS * OWN

    def to_x(dx):
        val = chip_sum(dx)
        cnt, sq = stats_of(val[:, WIDTH:])
        x_out[dx - 1, 0:span4, :] = val[:, 0:WIDTH].astype(BF16)
        tile = pack_stats(cnt, sq)
        x_out[dx - 1, span4 : span4 + 16, :] = tile[:, 0:WIDTH]
        x_out[dx - 1, span4 + 16 : span4 + 32, :] = tile[:, WIDTH:]
        remote(
            x_out.at[dx - 1], x_in.at[XS - dx - 1],
            r_send.at[3 + dx], r_recv.at[3 + XS - dx], x_peer[dx],
        )

    second_pass(3)
    to_sibling(0, 2, 4)
    second_pass(2)
    to_sibling(1, 1, 8)
    from_sibling(0, 2, 4)
    to_x(2)
    second_pass(1)
    from_sibling(1, 1, 8)
    to_x(1)
    to_x(3)
    second_pass(0)
    to_sibling(2, 0, 4)
    for dx in (1, 2, 3):
        ref = x_in.at[dx - 1]
        pltpu.make_async_copy(ref, ref, r_recv.at[3 + dx]).wait()
    from_sibling(2, 0, 4)

    val = chip_sum(0)
    tot = val[:, 0:WIDTH]
    cnt, sq = stats_of(val[:, WIDTH:])
    for i in range(XS - 1):
        tot = tot + x_in[i, 0:span4, :].astype(F32)
        tile = jnp.concatenate(
            [x_in[i, span4 : span4 + 16, :], x_in[i, span4 + 16 : span4 + 32, :]], axis=1
        ).astype(F32)
        cnt = cnt + tile[0:1, :] + tile[1:2, :] + tile[2:3, :]
        sq = sq + tile[3:4, :] + tile[4:5, :] + tile[5:6, :]
    tile = pack_stats(cnt, sq)
    for dz in (2, 1, 3):
        lanes = slice((dz // 2) * WIDTH, (dz // 2 + 1) * WIDTH)
        z_out[dz - 1, 0:OWN, :] = tot[dz * OWN : (dz + 1) * OWN, :].astype(BF16)
        z_out[dz - 1, OWN:BLOCK, :] = tile[:, lanes]
        remote(
            z_out.at[dz - 1], z_in.at[ZS - dz - 1],
            r_send.at[6 + dz], r_recv.at[6 + ZS - dz], z_peer[dz],
        )

    is_cnt = (row < 3) & (col < WIDTH)
    is_sq = (row >= 3) & (row < 6) & (col >= WIDTH)
    gather_stats = jnp.where(is_cnt | is_sq, 1.0, 0.0).astype(BF16)
    total = tot[0:OWN, :]
    stats = spread_rows(tile[:, 0:WIDTH], gather_stats)[0:OWN, :]
    for dz in (1, 3, 2):
        ref = z_in.at[dz - 1]
        pltpu.make_async_copy(ref, ref, r_recv.at[6 + dz]).wait()
    for dz in (1, 2, 3):
        half = ((ZS - dz) % 2) * OWN
        total = total + z_in[dz - 1, 0:OWN, :].astype(F32)
        stats = stats + spread_rows(z_in[dz - 1, OWN:BLOCK, :], gather_stats)[half : half + OWN, :]

    counts = stats[:, 0:WIDTH]
    squares = -2.0 * stats[:, WIDTH:]
    prior = means[...].astype(F32)
    prior_var = LOG2E / scale[0:OWN, :]
    denom = counts + 1.0
    centre = (total + prior) / denom
    cross = jnp.sum(centre * total, axis=1, keepdims=True)
    own_sq = jnp.sum(centre * centre, axis=1, keepdims=True)
    spread = (squares - 2.0 * cross + counts * own_sq + WIDTH * prior_var) / (WIDTH * denom)
    weight = jnp.log(denom / (total_points + COMPONENTS))
    out_means[...] = centre.astype(BF16)
    lane = lax.broadcasted_iota(jnp.int32, (OWN, WIDTH), 1)
    flat = jnp.where(lane == 0, spread, weight).T
    out_var[...] = flat[0:1, :]
    out_logw[...] = flat[1:2, :]

    for copy in sends:
        copy.wait_send()


def per_device(points, means, variances, log_weights):
    comps = lax.axis_size("comp")
    npoints = points.shape[0]
    own = means.shape[0]
    group = own * lax.axis_size("dp")
    vmem = pl.BlockSpec(memory_space=pltpu.VMEM)
    shape = jax.ShapeDtypeStruct
    new_means, new_var, new_logw, lik = pl.pallas_call(
        functools.partial(body, comps, npoints, npoints * lax.axis_size("dp")),
        out_shape=[
            shape((own, WIDTH), BF16),
            shape((1, own), F32),
            shape((1, own), F32),
            shape((1, npoints), F32),
        ],
        in_specs=[vmem] * 4,
        out_specs=[vmem] * 4,
        scratch_shapes=[
            pltpu.VMEM((32, BLOCK, WIDTH), BF16),
            pltpu.VMEM((group, 2 * WIDTH), BF16),
            pltpu.VMEM((group, WIDTH), F32),
            pltpu.VMEM((2 * WIDTH, npoints), BF16),
            pltpu.VMEM((npoints, 2 * WIDTH), BF16),
            pltpu.VMEM((group, npoints), F32),
            pltpu.VMEM((8, npoints), F32),
            pltpu.VMEM((8, npoints), F32),
            pltpu.VMEM((comps, 1, npoints), F32),
            pltpu.VMEM((group, 2 * WIDTH), F32),
            pltpu.VMEM((group // 2, 2 * WIDTH), F32),
            pltpu.VMEM((3, 4 * OWN + 32, WIDTH), BF16),
            pltpu.VMEM((3, 4 * OWN + 32, WIDTH), BF16),
            pltpu.VMEM((3, BLOCK, WIDTH), BF16),
            pltpu.VMEM((3, BLOCK, WIDTH), BF16),
            pltpu.SemaphoreType.DMA((32,)),
            pltpu.SemaphoreType.DMA((32,)),
            pltpu.SemaphoreType.DMA((8,)),
            pltpu.SemaphoreType.DMA((8,)),
            pltpu.SemaphoreType.DMA((10,)),
            pltpu.SemaphoreType.DMA((10,)),
        ],
        compiler_params=pltpu.CompilerParams(
            collective_id=0, has_side_effects=True, vmem_limit_bytes=60 << 20
        ),
        name="em_step",
    )(points, means, variances.reshape(1, own), log_weights.reshape(1, own))
    return new_means, new_var.reshape(own), new_logw.reshape(own), lik.reshape(npoints)


def solution(mesh):
    in_specs = (P("dp", None), P(("dp", "comp"), None), P(("dp", "comp")), P(("dp", "comp")))
    out_specs = (P(("dp", "comp"), None), P(("dp", "comp")), P(("dp", "comp")), P("dp"))
    return jax.shard_map(
        per_device, mesh=mesh, in_specs=in_specs, out_specs=out_specs, check_vma=False
    )
```

```python
import functools

import jax
import jax.numpy as jnp
from jax import lax
from jax.experimental import pallas as pl
from jax.experimental.pallas import tpu as pltpu
from jax.sharding import PartitionSpec as P

MESH = pl.DeviceIdType.MESH
F32 = jnp.float32
BF16 = jnp.bfloat16

COMPONENTS = 16384
LOG2E = 1.4426950408889634
LN2 = 0.6931471805599453
TWO_PI = 6.283185307179586

XS, ZS, CORES = 4, 4, 2
Z = 8
DEPTH = 4
WIDTH = 128
OWN = 64
BLOCK = 80
CHUNK = 512
TILE = 512
PARTS = 4

BASE = {
    (0, 0): 0, (1, 0): 4,
    (0, 1): 8, (0, 2): 12,
    (1, 1): 16, (1, 2): 20,
    (0, 3): 24, (1, 3): 28,
}
GROUP = XS * OWN


def split3(v):
    hi = v.astype(BF16).astype(F32)
    mid = (v - hi).astype(BF16).astype(F32)
    lo = (v - hi - mid).astype(BF16).astype(F32)
    return hi, mid, lo


def rows16(parts, lanes):
    row = lax.broadcasted_iota(jnp.int32, (16, lanes), 0)
    out = jnp.zeros((16, lanes), F32)
    for i, part in parts.items():
        out = jnp.where(row == i, jnp.broadcast_to(part, (16, lanes)), out)
    return out


def spread_rows(tile, table):
    return lax.dot_general(tile, table, (((0,), (0,)), ((), ())), preferred_element_type=F32)


def body(
    comps, npoints, total_points,
    points_hbm, means_hbm, var_hbm, logw_hbm,
    out_means, out_var, out_logw, out_lik,
    points, means, var, logw, blocks, centres, scale, pts_t, pts, prob, peak, mass, lse, sums,
    sib_out, sib, sib_stats_out, sib_stats, r_out, r_in,
    p_sem, g_send, g_recv, l_send, l_recv, s_send, s_recv, r_send, r_recv,
):
    dp = lax.axis_index("dp")
    cp = lax.axis_index("comp")
    core = dp % CORES
    zh = (dp // CORES) % ZS
    xx = dp // (CORES * ZS)
    zl = cp % 2
    yy = cp // 2
    zz = zh * 2 + zl
    sign = 1 - 2 * zl

    def device(dx, dz, dc=0):
        z = (zz + dz + Z) % Z
        return {
            "dp": ((xx + dx) % XS) * (ZS * CORES) + (z // 2) * CORES + (core + dc) % CORES,
            "comp": yy * 2 + z % 2,
        }

    def owner(dx, j, dc=0):
        return device(dx, -sign * j, dc)

    def user(dx, j, dc=0):
        return device(XS - dx, sign * j if j % 2 == 0 else -sign * j, dc)

    sibling = {"dp": dp + 1 - 2 * core}
    c_peer = {d: {"comp": (cp + d) % comps} for d in range(1, comps)}
    others = [(dx, j) for j in range(DEPTH) for dx in range(XS) if (dx, j) != (0, 0)]

    barrier = pltpu.get_barrier_semaphore()
    everyone = [sibling, *c_peer.values()]
    everyone += [owner(dx, j) for dx, j in others]
    everyone += [user(dx, 2) for dx in range(XS)]
    everyone += [owner(dx, 0, 1) for dx in range(1, XS)]
    for peer in everyone:
        pl.semaphore_signal(barrier, inc=1, device_id=peer, device_id_type=MESH)
    fetches = [
        pltpu.make_async_copy(src, dst, p_sem.at[i])
        for i, (src, dst) in enumerate(
            [(means_hbm, means), (var_hbm, var), (logw_hbm, logw), (points_hbm, points)]
        )
    ]
    for copy in fetches:
        copy.start()
    for copy in fetches[:3]:
        copy.wait()

    m = means[...]
    mf = m.astype(F32)
    msq = mf * mf
    msq_hi = msq.astype(BF16)
    msq_lo = (msq - msq_hi.astype(F32)).astype(BF16)
    ones = jnp.ones((16, WIDTH), BF16)
    nt = (((1,), (1,)), ((), ()))
    centre_sq = (
        lax.dot_general(ones, msq_hi, nt, preferred_element_type=F32)
        + lax.dot_general(ones, msq_lo, nt, preferred_element_type=F32)
    )[0:1, :]
    v = var[...]
    offset = logw[...] - 0.5 * WIDTH * jnp.log(TWO_PI * v)
    e_hi, e_mid, e_lo = split3(v * offset - 0.5 * centre_sq)
    a_hi, a_mid, a_lo = split3(LOG2E / v)
    blocks[0, 0:OWN, :] = m
    blocks[0, OWN:BLOCK, :] = jnp.zeros((16, WIDTH), BF16)
    blocks[0, OWN:BLOCK, 0:OWN] = rows16(
        {0: e_hi, 1: e_mid, 2: e_lo, 3: a_hi, 4: a_mid, 5: a_lo, 6: jnp.ones_like(v)}, OWN
    ).astype(BF16)

    pts_t[WIDTH + 16 : 2 * WIDTH, :] = jnp.zeros((WIDTH - 16, npoints), BF16)
    row16 = lax.broadcasted_iota(jnp.int32, (16, WIDTH), 0)
    col16 = lax.broadcasted_iota(jnp.int32, (16, WIDTH), 1)
    eye16 = jnp.where(row16 == col16, 1.0, 0.0).astype(BF16)

    def prepare(j, carry):
        for u in range(4):
            at = pl.ds(pl.multiple_of((j * 4 + u) * WIDTH, WIDTH), WIDTH)
            x = points[at, :]
            xt = x.astype(F32).T
            half = -0.5 * jnp.sum(xt * xt, axis=0, keepdims=True)
            b_hi, b_mid, b_lo = split3(half)
            one = jnp.ones_like(half)
            tile = rows16({0: one, 1: one, 2: one, 3: b_hi, 4: b_mid, 5: b_lo}, WIDTH).astype(BF16)
            pts_t[0:WIDTH, at] = xt.astype(BF16)
            pts_t[WIDTH : WIDTH + 16, at] = tile
            pts[at, 0:WIDTH] = x
            pts[at, WIDTH : 2 * WIDTH] = lax.dot_general(
                tile, eye16, (((0,), (0,)), ((), ())), preferred_element_type=F32
            ).astype(BF16)
        return carry

    fetches[3].wait()
    steps = npoints // WIDTH // 4
    lax.fori_loop(0, steps // 2, prepare, 0)

    pl.semaphore_wait(barrier, len(everyone))

    sends = []

    def remote(src, dst, send, recv, peer):
        copy = pltpu.make_async_remote_copy(
            src_ref=src, dst_ref=dst, send_sem=send, recv_sem=recv,
            device_id=peer, device_id_type=MESH,
        )
        copy.start()
        sends.append(copy)

    def arrived(ref, sem):
        pltpu.make_async_copy(ref, ref, sem).wait()

    counter = [0]

    def gather_send(src, dst, n, peer):
        i = counter[0]
        counter[0] += 1
        remote(
            blocks.at[pl.ds(src, n)], blocks.at[pl.ds(dst, n)],
            g_send.at[i], g_recv.at[dst], peer,
        )

    def gather_wait(slot, n):
        arrived(blocks.at[pl.ds(slot, n)], g_recv.at[slot])

    gather_send(0, BASE[1, 0], 1, sibling)
    for dx in (2, 1, 3):
        gather_send(0, BASE[0, 0] + dx, 1, user(dx, 0))
        gather_send(0, BASE[1, 0] + dx, 1, user(dx, 0, 1))
    for j in (1, 2, 3):
        for dx in (2, 1, 3, 0):
            gather_send(0, BASE[0, j] + dx, 1, user(dx, j))

    lax.fori_loop(steps // 2, steps, prepare, 0)

    row = lax.broadcasted_iota(jnp.int32, (16, 2 * WIDTH), 0)
    col = lax.broadcasted_iota(jnp.int32, (16, 2 * WIDTH), 1)
    put = ((row < 3) & (col == row)) | ((row == 6) & (col >= 3) & (col < 6))
    put = put | ((row >= 3) & (row < 6) & (col >= WIDTH))
    table = jnp.where(put, 1.0, 0.0).astype(BF16)

    def expand(first, n):
        for s in range(first, first + n):
            at = slice(s * OWN, (s + 1) * OWN)
            wide = spread_rows(blocks[s, OWN:BLOCK, :], table)[0:OWN, :]
            centres[at, 0:WIDTH] = blocks[s, 0:OWN, :]
            centres[at, WIDTH : 2 * WIDTH] = wide[:, 0:WIDTH].astype(BF16)
            scale[at, :] = wide[:, WIDTH : 2 * WIDTH]

    def first_pass(c, first, last):
        at = slice(c * CHUNK, (c + 1) * CHUNK)
        for t in range(first // TILE, last // TILE):
            ns = slice(t * TILE, (t + 1) * TILE)
            y = jnp.dot(centres[at, :], pts_t[:, ns], preferred_element_type=F32)
            y = y * jnp.concatenate([scale[at, :]] * (TILE // WIDTH), axis=1)
            top = jnp.max(y, axis=0, keepdims=True)
            p = jnp.exp2(y - top)
            prob[at, ns] = p
            peak[c : c + 1, ns] = top
            mass[c : c + 1, ns] = jnp.sum(p, axis=0, keepdims=True)

    chunks = 4
    part = npoints // PARTS
    parts = [slice(h * part, (h + 1) * part) for h in range(PARTS)]

    def lse_send(h):
        ns = parts[h]
        top = jnp.max(peak[0:chunks, ns], axis=0, keepdims=True)
        total = jnp.sum(mass[0:chunks, ns] * jnp.exp2(peak[0:chunks, ns] - top), axis=0, keepdims=True)
        lse[h, 0] = top + jnp.log(total) * LOG2E
        for d in range(1, comps):
            remote(
                lse.at[h, 0], lse.at[h, comps - d],
                l_send.at[h, d], l_recv.at[h, comps - d], c_peer[d],
            )

    def lse_finish(h):
        ns = parts[h]
        for d in range(1, comps):
            arrived(lse.at[h, d], l_recv.at[h, d])
        top = lse[h, 0]
        for d in range(1, comps):
            top = jnp.maximum(top, lse[h, d])
        total = jnp.exp2(lse[h, 0] - top)
        for d in range(1, comps):
            total = total + jnp.exp2(lse[h, d] - top)
        lik = top + jnp.log(total) * LOG2E
        out_lik[:, ns] = lik * LN2
        for c in range(chunks):
            peak[c : c + 1, ns] = jnp.exp2(peak[c : c + 1, ns] - lik)

    for dx in range(XS):
        if dx:
            gather_wait(BASE[0, 0] + dx, 1)
        gather_wait(BASE[1, 0] + dx, 1)
    expand(0, 8)
    first_pass(0, 0, npoints)
    for j in (1, 2):
        for dx in range(XS):
            gather_wait(BASE[0, j] + dx, 1)
        gather_send(BASE[0, j], BASE[1, j], XS, sibling)
    expand(8, 8)
    first_pass(1, 0, npoints)
    for dx in range(XS):
        gather_wait(BASE[0, 3] + dx, 1)
    gather_send(BASE[0, 3], BASE[1, 3], XS, sibling)
    gather_wait(BASE[1, 1], XS)
    gather_wait(BASE[1, 2], XS)
    expand(16, 12)
    for h in range(PARTS):
        first_pass(2, parts[h].start, parts[h].stop)
        if h == 0:
            gather_wait(BASE[1, 3], XS)
            expand(28, 4)
        first_pass(3, parts[h].start, parts[h].stop)
        lse_send(h)

    def second_pass(h, groups):
        ns = parts[h]
        p = []
        for g in groups:
            first = BASE[g] * OWN
            c = first // CHUNK
            p.append((prob[first : first + GROUP, ns] * peak[c : c + 1, ns]).astype(BF16))
        acc = jnp.dot(jnp.concatenate(p, axis=0), pts[ns, :], preferred_element_type=F32)
        for i, g in enumerate(groups):
            at = slice(BASE[g] * OWN, BASE[g] * OWN + GROUP)
            val = acc[i * GROUP : (i + 1) * GROUP, :]
            val = val if h == 0 else sums[at, :] + val
            sums[at, :] = val
            if h == PARTS - 1 and g[0] == 1:
                sib_out[g[1]] = val[:, 0:WIDTH]
                sib_stats_out[g[1]] = val[:, WIDTH:].T[0:8, :]

    def to_sibling(j):
        remote(sib_out.at[j], sib.at[j], s_send.at[0, j], s_recv.at[0, j], sibling)
        remote(sib_stats_out.at[j], sib_stats.at[j], s_send.at[1, j], s_recv.at[1, j], sibling)

    def pack_stats(cnt, sq):
        c_hi, c_mid, c_lo = split3(cnt)
        s_hi, s_mid, s_lo = split3(sq)
        parts = {0: c_hi, 1: c_mid, 2: c_lo, 3: s_hi, 4: s_mid, 5: s_lo}
        return rows16(parts, cnt.shape[1]).astype(BF16)

    def chip_sum(j):
        at = slice(BASE[0, j] * OWN, BASE[0, j] * OWN + GROUP)
        t = sums[at, WIDTH:].T[0:8, :]
        arrived(sib.at[j], s_recv.at[0, j])
        arrived(sib_stats.at[j], s_recv.at[1, j])
        t = t + sib_stats[j]
        return sums[at, 0:WIDTH] + sib[j], t[0:1, :], t[3:4, :] + t[4:5, :] + t[5:6, :]

    def to_owner(j):
        tot, cnt, sq = chip_sum(j)
        tile = pack_stats(cnt, sq)
        for dx in (2, 1, 3, 0):
            if (dx, j) == (0, 0):
                continue
            r_out[j, dx, 0:OWN, :] = tot[dx * OWN : (dx + 1) * OWN, :].astype(BF16)
            r_out[j, dx, OWN:BLOCK, :] = tile[:, (dx // 2) * WIDTH : (dx // 2 + 1) * WIDTH]
            remote(
                r_out.at[j, dx], r_in.at[j, dx], r_send.at[j, dx], r_recv.at[j, dx], owner(dx, j)
            )
        return tot[0:OWN, :], cnt[:, 0:WIDTH], sq[:, 0:WIDTH]

    steps = [[(1, 3), (1, 2)], [(1, 1), (1, 0)], [(0, 3), (0, 2)], [(0, 1), (0, 0)]]
    for h in range(PARTS - 1):
        lse_finish(h)
        for step in steps:
            second_pass(h, step)
    lse_finish(PARTS - 1)
    second_pass(PARTS - 1, steps[0])
    to_sibling(3)
    to_sibling(2)
    second_pass(PARTS - 1, steps[1])
    to_sibling(1)
    to_sibling(0)
    second_pass(PARTS - 1, steps[2])
    second_pass(PARTS - 1, steps[3])
    to_owner(3)
    to_owner(2)
    to_owner(1)
    total, cnt, sq = to_owner(0)

    tiles = [None, None]
    for dx, j in sorted(others, key=lambda o: -o[1]):
        arrived(r_in.at[j, dx], r_recv.at[j, dx])
        total = total + r_in[j, dx, 0:OWN, :].astype(F32)
        tile = r_in[j, dx, OWN:BLOCK, :].astype(F32)
        tiles[dx % 2] = tile if tiles[dx % 2] is None else tiles[dx % 2] + tile
    is_cnt = (row < 3) & (col < WIDTH)
    is_sq = (row >= 3) & (row < 6) & (col >= WIDTH)
    columns = jnp.where(is_cnt | is_sq, 1.0, 0.0).astype(BF16)
    stats = 0.0
    for odd in (0, 1):
        t = tiles[odd]
        c = t[0:1, :] + t[1:2, :] + t[2:3, :]
        s = t[3:4, :] + t[4:5, :] + t[5:6, :]
        if not odd:
            c, s = c + cnt, s + sq
        wide = spread_rows(pack_stats(c, s), columns)
        stats = stats + wide[odd * OWN : (odd + 1) * OWN, :]

    counts = stats[:, 0:WIDTH]
    squares = -2.0 * stats[:, WIDTH:]
    prior = means[...].astype(F32)
    prior_var = LOG2E / scale[0:OWN, :]
    denom = counts + 1.0
    centre = (total + prior) / denom
    cross = jnp.sum(centre * total, axis=1, keepdims=True)
    own_sq = jnp.sum(centre * centre, axis=1, keepdims=True)
    spread = (squares - 2.0 * cross + counts * own_sq + WIDTH * prior_var) / (WIDTH * denom)
    weight = jnp.log(denom / (total_points + COMPONENTS))
    out_means[...] = centre.astype(BF16)
    lane = lax.broadcasted_iota(jnp.int32, (OWN, WIDTH), 1)
    flat = jnp.where(lane == 0, spread, weight).T
    out_var[...] = flat[0:1, :]
    out_logw[...] = flat[1:2, :]

    for copy in sends:
        copy.wait_send()


def finish(*refs):
    for src, dst in zip(refs[:4], refs[4:]):
        dst[...] = src[...]


def per_device(points, means, variances, log_weights):
    comps = lax.axis_size("comp")
    npoints = points.shape[0]
    own = means.shape[0]
    group = own * lax.axis_size("dp")
    vmem = pl.BlockSpec(memory_space=pltpu.VMEM)
    shape = jax.ShapeDtypeStruct
    dma = pltpu.SemaphoreType.DMA
    results = pl.pallas_call(
        functools.partial(body, comps, npoints, npoints * lax.axis_size("dp")),
        out_shape=[
            shape((own, WIDTH), BF16),
            shape((1, own), F32),
            shape((1, own), F32),
            shape((1, npoints), F32),
        ],
        in_specs=[pl.BlockSpec(memory_space=pl.ANY)] * 4,
        out_specs=[vmem] * 4,
        scratch_shapes=[
            pltpu.VMEM((npoints, WIDTH), BF16),
            pltpu.VMEM((own, WIDTH), BF16),
            pltpu.VMEM((1, own), F32),
            pltpu.VMEM((1, own), F32),
            pltpu.VMEM((32, BLOCK, WIDTH), BF16),
            pltpu.VMEM((group, 2 * WIDTH), BF16),
            pltpu.VMEM((group, WIDTH), F32),
            pltpu.VMEM((2 * WIDTH, npoints), BF16),
            pltpu.VMEM((npoints, 2 * WIDTH), BF16),
            pltpu.VMEM((group, npoints), F32),
            pltpu.VMEM((8, npoints), F32),
            pltpu.VMEM((8, npoints), F32),
            pltpu.VMEM((PARTS, comps, 1, npoints // PARTS), F32),
            pltpu.VMEM((group, 2 * WIDTH), F32),
            pltpu.VMEM((DEPTH, GROUP, WIDTH), F32),
            pltpu.VMEM((DEPTH, GROUP, WIDTH), F32),
            pltpu.VMEM((DEPTH, 8, GROUP), F32),
            pltpu.VMEM((DEPTH, 8, GROUP), F32),
            pltpu.VMEM((DEPTH, XS, BLOCK, WIDTH), BF16),
            pltpu.VMEM((DEPTH, XS, BLOCK, WIDTH), BF16),
            dma((4,)),
            dma((32,)),
            dma((32,)),
            dma((PARTS, comps)),
            dma((PARTS, comps)),
            dma((2, DEPTH)),
            dma((2, DEPTH)),
            dma((DEPTH, XS)),
            dma((DEPTH, XS)),
        ],
        compiler_params=pltpu.CompilerParams(
            collective_id=0, has_side_effects=True, vmem_limit_bytes=60 << 20
        ),
        name="em_step",
    )(points, means, variances.reshape(1, own), log_weights.reshape(1, own))
    new_means, new_var, new_logw, lik = pl.pallas_call(
        finish,
        out_shape=[
            shape((own, WIDTH), BF16),
            shape((1, own), F32),
            shape((1, own), F32),
            shape((1, npoints), F32),
        ],
        in_specs=[vmem] * 4,
        out_specs=[vmem] * 4,
        name="results",
    )(*results)
    return new_means, new_var.reshape(own), new_logw.reshape(own), lik.reshape(npoints)


def solution(mesh):
    in_specs = (P("dp", None), P(("dp", "comp"), None), P(("dp", "comp")), P(("dp", "comp")))
    out_specs = (P(("dp", "comp"), None), P(("dp", "comp")), P(("dp", "comp")), P("dp"))
    return jax.shard_map(
        per_device, mesh=mesh, in_specs=in_specs, out_specs=out_specs, check_vma=False
    )
```

```python
import functools

import jax
import jax.numpy as jnp
from jax import lax
from jax.experimental import pallas as pl
from jax.experimental.pallas import tpu as pltpu
from jax.sharding import PartitionSpec as P

MESH = pl.DeviceIdType.MESH
F32 = jnp.float32
BF16 = jnp.bfloat16

COMPONENTS = 16384
LOG2E = 1.4426950408889634
LN2 = 0.6931471805599453
TWO_PI = 6.283185307179586

XS, ZS, CORES = 4, 4, 2
Z = 8
DEPTH = 4
WIDTH = 128
OWN = 64
BLOCK = 80
CHUNK = 512
TILE = 512
PARTS = 2

BASE = {
    (0, 0): 0, (1, 0): 4,
    (0, 1): 8, (0, 2): 12,
    (1, 1): 16, (1, 2): 20,
    (0, 3): 24, (1, 3): 28,
}
GROUP = XS * OWN


def split3(v):
    hi = v.astype(BF16).astype(F32)
    mid = (v - hi).astype(BF16).astype(F32)
    lo = (v - hi - mid).astype(BF16).astype(F32)
    return hi, mid, lo


def rows16(parts, lanes):
    row = lax.broadcasted_iota(jnp.int32, (16, lanes), 0)
    out = jnp.zeros((16, lanes), F32)
    for i, part in parts.items():
        out = jnp.where(row == i, jnp.broadcast_to(part, (16, lanes)), out)
    return out


def spread_rows(tile, table):
    return lax.dot_general(tile, table, (((0,), (0,)), ((), ())), preferred_element_type=F32)


def body(
    comps, npoints, total_points,
    points_hbm, means_hbm, var_hbm, logw_hbm,
    out_means, out_var, out_logw, out_lik,
    points, means, var, logw, blocks, centres, scale, pts_t, pts, prob, peak, mass, lse, sums,
    sib_out, sib, sib_stats_out, sib_stats, r_out, r_in,
    p_sem, g_send, g_recv, l_send, l_recv, s_send, s_recv, r_send, r_recv,
):
    dp = lax.axis_index("dp")
    cp = lax.axis_index("comp")
    core = dp % CORES
    zh = (dp // CORES) % ZS
    xx = dp // (CORES * ZS)
    zl = cp % 2
    yy = cp // 2
    zz = zh * 2 + zl
    sign = 1 - 2 * zl

    def device(dx, dz, dc=0):
        z = (zz + dz + Z) % Z
        return {
            "dp": ((xx + dx) % XS) * (ZS * CORES) + (z // 2) * CORES + (core + dc) % CORES,
            "comp": yy * 2 + z % 2,
        }

    def owner(dx, j, dc=0):
        return device(dx, -sign * j, dc)

    def user(dx, j, dc=0):
        return device(XS - dx, sign * j if j % 2 == 0 else -sign * j, dc)

    sibling = {"dp": dp + 1 - 2 * core}
    c_peer = {d: {"comp": (cp + d) % comps} for d in range(1, comps)}
    others = [(dx, j) for j in range(DEPTH - 1) for dx in range(XS) if (dx, j) != (0, 0)]
    far = DEPTH - 1
    others.append((0, far))

    barrier = pltpu.get_barrier_semaphore()
    everyone = [sibling, *c_peer.values()]
    everyone += [owner(dx, j) for dx, j in others]
    everyone += [user(dx, 2) for dx in range(XS)]
    everyone += [owner(dx, 0, 1) for dx in range(1, XS)]
    for peer in everyone:
        pl.semaphore_signal(barrier, inc=1, device_id=peer, device_id_type=MESH)
    fetches = [
        pltpu.make_async_copy(src, dst, p_sem.at[i])
        for i, (src, dst) in enumerate(
            [(means_hbm, means), (var_hbm, var), (logw_hbm, logw), (points_hbm, points)]
        )
    ]
    for copy in fetches:
        copy.start()
    for copy in fetches[:3]:
        copy.wait()

    m = means[...]
    mf = m.astype(F32)
    msq = mf * mf
    msq_hi = msq.astype(BF16)
    msq_lo = (msq - msq_hi.astype(F32)).astype(BF16)
    ones = jnp.ones((16, WIDTH), BF16)
    nt = (((1,), (1,)), ((), ()))
    centre_sq = (
        lax.dot_general(ones, msq_hi, nt, preferred_element_type=F32)
        + lax.dot_general(ones, msq_lo, nt, preferred_element_type=F32)
    )[0:1, :]
    v = var[...]
    offset = logw[...] - 0.5 * WIDTH * jnp.log(TWO_PI * v)
    e_hi, e_mid, e_lo = split3(v * offset - 0.5 * centre_sq)
    a_hi, a_mid, a_lo = split3(LOG2E / v)
    blocks[0, 0:OWN, :] = m
    blocks[0, OWN:BLOCK, :] = jnp.zeros((16, WIDTH), BF16)
    blocks[0, OWN:BLOCK, 0:OWN] = rows16(
        {0: e_hi, 1: e_mid, 2: e_lo, 3: a_hi, 4: a_mid, 5: a_lo, 6: jnp.ones_like(v)}, OWN
    ).astype(BF16)

    pts_t[WIDTH + 16 : 2 * WIDTH, :] = jnp.zeros((WIDTH - 16, npoints), BF16)
    row16 = lax.broadcasted_iota(jnp.int32, (16, WIDTH), 0)
    col16 = lax.broadcasted_iota(jnp.int32, (16, WIDTH), 1)
    eye16 = jnp.where(row16 == col16, 1.0, 0.0).astype(BF16)

    def prepare(j, carry):
        for u in range(4):
            at = pl.ds(pl.multiple_of((j * 4 + u) * WIDTH, WIDTH), WIDTH)
            x = points[at, :]
            xt = x.astype(F32).T
            half = -0.5 * jnp.sum(xt * xt, axis=0, keepdims=True)
            b_hi, b_mid, b_lo = split3(half)
            one = jnp.ones_like(half)
            tile = rows16({0: one, 1: one, 2: one, 3: b_hi, 4: b_mid, 5: b_lo}, WIDTH).astype(BF16)
            pts_t[0:WIDTH, at] = xt.astype(BF16)
            pts_t[WIDTH : WIDTH + 16, at] = tile
            pts[at, 0:WIDTH] = x
            pts[at, WIDTH : 2 * WIDTH] = lax.dot_general(
                tile, eye16, (((0,), (0,)), ((), ())), preferred_element_type=F32
            ).astype(BF16)
        return carry

    fetches[3].wait()
    steps = npoints // WIDTH // 4
    lax.fori_loop(0, steps // 2, prepare, 0)

    pl.semaphore_wait(barrier, len(everyone))

    sends = []

    def remote(src, dst, send, recv, peer):
        copy = pltpu.make_async_remote_copy(
            src_ref=src, dst_ref=dst, send_sem=send, recv_sem=recv,
            device_id=peer, device_id_type=MESH,
        )
        copy.start()
        sends.append(copy)

    def arrived(ref, sem):
        pltpu.make_async_copy(ref, ref, sem).wait()

    counter = [0]

    def gather_send(src, dst, n, peer):
        i = counter[0]
        counter[0] += 1
        remote(
            blocks.at[pl.ds(src, n)], blocks.at[pl.ds(dst, n)],
            g_send.at[i], g_recv.at[dst], peer,
        )

    def gather_wait(slot, n):
        arrived(blocks.at[pl.ds(slot, n)], g_recv.at[slot])

    gather_send(0, BASE[1, 0], 1, sibling)
    for dx in (2, 1, 3):
        gather_send(0, BASE[0, 0] + dx, 1, user(dx, 0))
        gather_send(0, BASE[1, 0] + dx, 1, user(dx, 0, 1))
    gather_send(0, BASE[0, far], 1, user(0, far))
    for j in (1, 2):
        for dx in (2, 1, 3, 0):
            gather_send(0, BASE[0, j] + dx, 1, user(dx, j))

    lax.fori_loop(steps // 2, steps, prepare, 0)

    row = lax.broadcasted_iota(jnp.int32, (16, 2 * WIDTH), 0)
    col = lax.broadcasted_iota(jnp.int32, (16, 2 * WIDTH), 1)
    put = ((row < 3) & (col == row)) | ((row == 6) & (col >= 3) & (col < 6))
    put = put | ((row >= 3) & (row < 6) & (col >= WIDTH))
    table = jnp.where(put, 1.0, 0.0).astype(BF16)

    def expand(first, n):
        for s in range(first, first + n):
            at = slice(s * OWN, (s + 1) * OWN)
            wide = spread_rows(blocks[s, OWN:BLOCK, :], table)[0:OWN, :]
            centres[at, 0:WIDTH] = blocks[s, 0:OWN, :]
            centres[at, WIDTH : 2 * WIDTH] = wide[:, 0:WIDTH].astype(BF16)
            scale[at, :] = wide[:, WIDTH : 2 * WIDTH]

    def first_pass(c, first, last):
        at = slice(c * CHUNK, (c + 1) * CHUNK)
        for t in range(first // TILE, last // TILE):
            ns = slice(t * TILE, (t + 1) * TILE)
            y = jnp.dot(centres[at, :], pts_t[:, ns], preferred_element_type=F32)
            y = y * jnp.concatenate([scale[at, :]] * (TILE // WIDTH), axis=1)
            top = jnp.max(y, axis=0, keepdims=True)
            p = jnp.exp2(y - top)
            prob[at, ns] = p
            peak[c : c + 1, ns] = top
            mass[c : c + 1, ns] = jnp.sum(p, axis=0, keepdims=True)

    chunks = 4
    part = npoints // PARTS
    parts = [slice(h * part, (h + 1) * part) for h in range(PARTS)]

    def lse_send(h):
        ns = parts[h]
        top = jnp.max(peak[0:chunks, ns], axis=0, keepdims=True)
        total = jnp.sum(mass[0:chunks, ns] * jnp.exp2(peak[0:chunks, ns] - top), axis=0, keepdims=True)
        lse[h, 0] = top + jnp.log(total) * LOG2E
        for d in range(1, comps):
            remote(
                lse.at[h, 0], lse.at[h, comps - d],
                l_send.at[h, d], l_recv.at[h, comps - d], c_peer[d],
            )

    def lse_finish(h):
        ns = parts[h]
        for d in range(1, comps):
            arrived(lse.at[h, d], l_recv.at[h, d])
        top = lse[h, 0]
        for d in range(1, comps):
            top = jnp.maximum(top, lse[h, d])
        total = jnp.exp2(lse[h, 0] - top)
        for d in range(1, comps):
            total = total + jnp.exp2(lse[h, d] - top)
        lik = top + jnp.log(total) * LOG2E
        out_lik[:, ns] = lik * LN2
        for c in range(chunks):
            peak[c : c + 1, ns] = jnp.exp2(peak[c : c + 1, ns] - lik)

    for dx in range(XS):
        if dx:
            gather_wait(BASE[0, 0] + dx, 1)
        gather_wait(BASE[1, 0] + dx, 1)
    expand(0, 8)
    first_pass(0, 0, npoints)
    gather_wait(BASE[0, far], 1)
    for d in (2, 1, 3):
        gather_send(BASE[0, far], BASE[0, far] + XS - d, 1, device(d, 0))
    for j in (1, 2):
        for dx in range(XS):
            gather_wait(BASE[0, j] + dx, 1)
        gather_send(BASE[0, j], BASE[1, j], XS, sibling)
    expand(8, 8)
    first_pass(1, 0, npoints)
    for dx in range(1, XS):
        gather_wait(BASE[0, far] + dx, 1)
    gather_send(BASE[0, far], BASE[1, far], XS, sibling)
    gather_wait(BASE[1, 1], XS)
    gather_wait(BASE[1, 2], XS)
    expand(16, 12)
    for h in range(PARTS):
        first_pass(2, parts[h].start, parts[h].stop)
        if h == 0:
            gather_wait(BASE[1, far], XS)
            expand(28, 4)
        first_pass(3, parts[h].start, parts[h].stop)
        lse_send(h)

    def second_pass(h, groups):
        ns = parts[h]
        p = []
        for g in groups:
            first = BASE[g] * OWN
            c = first // CHUNK
            p.append((prob[first : first + GROUP, ns] * peak[c : c + 1, ns]).astype(BF16))
        acc = jnp.dot(jnp.concatenate(p, axis=0), pts[ns, :], preferred_element_type=F32)
        for i, g in enumerate(groups):
            at = slice(BASE[g] * OWN, BASE[g] * OWN + GROUP)
            val = acc[i * GROUP : (i + 1) * GROUP, :]
            val = val if h == 0 else sums[at, :] + val
            sums[at, :] = val
            if h == PARTS - 1 and g[0] == 1:
                sib_out[g[1]] = val[:, 0:WIDTH]
                sib_stats_out[g[1]] = val[:, WIDTH:].T[0:8, :]

    def to_sibling(j):
        remote(sib_out.at[j], sib.at[j], s_send.at[0, j], s_recv.at[0, j], sibling)
        remote(sib_stats_out.at[j], sib_stats.at[j], s_send.at[1, j], s_recv.at[1, j], sibling)

    def pack_stats(cnt, sq):
        c_hi, c_mid, c_lo = split3(cnt)
        s_hi, s_mid, s_lo = split3(sq)
        parts = {0: c_hi, 1: c_mid, 2: c_lo, 3: s_hi, 4: s_mid, 5: s_lo}
        return rows16(parts, cnt.shape[1]).astype(BF16)

    def chip_sum(j):
        at = slice(BASE[0, j] * OWN, BASE[0, j] * OWN + GROUP)
        t = sums[at, WIDTH:].T[0:8, :]
        arrived(sib.at[j], s_recv.at[0, j])
        arrived(sib_stats.at[j], s_recv.at[1, j])
        t = t + sib_stats[j]
        return sums[at, 0:WIDTH] + sib[j], t[0:1, :], t[3:4, :] + t[4:5, :] + t[5:6, :]

    def packet(j, dx, tot, tile):
        r_out[j, dx, 0:OWN, :] = tot.astype(BF16)
        r_out[j, dx, OWN:BLOCK, :] = tile

    def send_packet(j, dx, slot, peer):
        remote(r_out.at[j, dx], r_in.at[j, slot], r_send.at[j, dx], r_recv.at[j, slot], peer)

    def to_owner(j):
        tot, cnt, sq = chip_sum(j)
        tile = pack_stats(cnt, sq)
        for dx in (2, 1, 3, 0):
            if dx == 0 and j in (0, far):
                continue
            lanes = slice((dx // 2) * WIDTH, (dx // 2 + 1) * WIDTH)
            packet(j, dx, tot[dx * OWN : (dx + 1) * OWN, :], tile[:, lanes])
            if j == far:
                send_packet(j, dx, XS - dx, device(dx, 0))
            else:
                send_packet(j, dx, dx, owner(dx, j))
        return tot[0:OWN, :], cnt[:, 0:WIDTH], sq[:, 0:WIDTH]

    def rows_of(tile):
        t = tile.astype(F32)
        return t[0:1, :] + t[1:2, :] + t[2:3, :], t[3:4, :] + t[4:5, :] + t[5:6, :]

    def add_packets(total, even, odd, slots):
        even, odd = list(even), [jnp.zeros_like(e) if odd is None else o for e, o in zip(even, odd or even)]
        for j, dx in slots:
            arrived(r_in.at[j, dx], r_recv.at[j, dx])
            total = total + r_in[j, dx, 0:OWN, :].astype(F32)
            got = rows_of(r_in[j, dx, OWN:BLOCK, :])
            if dx % 2 == 0:
                even = [a + b for a, b in zip(even, got)]
            if dx % 2 == 1 or (j, dx) == (far, 0):
                odd = [a + b for a, b in zip(odd, got)]
        return total, even, odd

    steps = [[(1, 3), (1, 2)], [(0, 3), (0, 2)], [(1, 1), (1, 0)], [(0, 1), (0, 0)]]
    for h in range(PARTS - 1):
        lse_finish(h)
        for step in steps:
            second_pass(h, step)
    lse_finish(PARTS - 1)
    second_pass(PARTS - 1, steps[0])
    to_sibling(3)
    to_sibling(2)
    second_pass(PARTS - 1, steps[1])
    second_pass(PARTS - 1, steps[2])
    to_sibling(1)
    to_sibling(0)
    total, *even = to_owner(far)
    to_owner(2)
    second_pass(PARTS - 1, steps[3])
    to_owner(1)
    own_total, *own_even = to_owner(0)
    total, even, odd = add_packets(total, even, None, [(far, dx) for dx in range(1, XS)])
    lane = lax.broadcasted_iota(jnp.int32, (1, WIDTH), 1)
    packet(far, 0, total, pack_stats(*[jnp.where(lane < OWN, a, b) for a, b in zip(even, odd)]))
    send_packet(far, 0, 0, owner(0, far))
    slots = [(j, dx) for j in range(far) for dx in range(XS) if (j, dx) != (0, 0)]
    total, even, odd = add_packets(own_total, own_even, None, slots + [(far, 0)])

    is_cnt = (row < 3) & (col < WIDTH)
    is_sq = (row >= 3) & (row < 6) & (col >= WIDTH)
    columns = jnp.where(is_cnt | is_sq, 1.0, 0.0).astype(BF16)
    stats = 0.0
    for i, rows in enumerate((even, odd)):
        wide = spread_rows(pack_stats(*rows), columns)
        stats = stats + wide[i * OWN : (i + 1) * OWN, :]

    counts = stats[:, 0:WIDTH]
    squares = -2.0 * stats[:, WIDTH:]
    prior = means[...].astype(F32)
    prior_var = LOG2E / scale[0:OWN, :]
    denom = counts + 1.0
    centre = (total + prior) / denom
    cross = jnp.sum(centre * total, axis=1, keepdims=True)
    own_sq = jnp.sum(centre * centre, axis=1, keepdims=True)
    spread = (squares - 2.0 * cross + counts * own_sq + WIDTH * prior_var) / (WIDTH * denom)
    weight = jnp.log(denom / (total_points + COMPONENTS))
    out_means[...] = centre.astype(BF16)
    lane = lax.broadcasted_iota(jnp.int32, (OWN, WIDTH), 1)
    flat = jnp.where(lane == 0, spread, weight).T
    out_var[...] = flat[0:1, :]
    out_logw[...] = flat[1:2, :]

    for copy in sends:
        copy.wait_send()


def finish(*refs):
    for src, dst in zip(refs[:4], refs[4:]):
        dst[...] = src[...]


def per_device(points, means, variances, log_weights):
    comps = lax.axis_size("comp")
    npoints = points.shape[0]
    own = means.shape[0]
    group = own * lax.axis_size("dp")
    vmem = pl.BlockSpec(memory_space=pltpu.VMEM)
    shape = jax.ShapeDtypeStruct
    dma = pltpu.SemaphoreType.DMA
    results = pl.pallas_call(
        functools.partial(body, comps, npoints, npoints * lax.axis_size("dp")),
        out_shape=[
            shape((own, WIDTH), BF16),
            shape((1, own), F32),
            shape((1, own), F32),
            shape((1, npoints), F32),
        ],
        in_specs=[pl.BlockSpec(memory_space=pl.ANY)] * 4,
        out_specs=[vmem] * 4,
        scratch_shapes=[
            pltpu.VMEM((npoints, WIDTH), BF16),
            pltpu.VMEM((own, WIDTH), BF16),
            pltpu.VMEM((1, own), F32),
            pltpu.VMEM((1, own), F32),
            pltpu.VMEM((32, BLOCK, WIDTH), BF16),
            pltpu.VMEM((group, 2 * WIDTH), BF16),
            pltpu.VMEM((group, WIDTH), F32),
            pltpu.VMEM((2 * WIDTH, npoints), BF16),
            pltpu.VMEM((npoints, 2 * WIDTH), BF16),
            pltpu.VMEM((group, npoints), F32),
            pltpu.VMEM((8, npoints), F32),
            pltpu.VMEM((8, npoints), F32),
            pltpu.VMEM((PARTS, comps, 1, npoints // PARTS), F32),
            pltpu.VMEM((group, 2 * WIDTH), F32),
            pltpu.VMEM((DEPTH, GROUP, WIDTH), F32),
            pltpu.VMEM((DEPTH, GROUP, WIDTH), F32),
            pltpu.VMEM((DEPTH, 8, GROUP), F32),
            pltpu.VMEM((DEPTH, 8, GROUP), F32),
            pltpu.VMEM((DEPTH, XS, BLOCK, WIDTH), BF16),
            pltpu.VMEM((DEPTH, XS, BLOCK, WIDTH), BF16),
            dma((4,)),
            dma((32,)),
            dma((32,)),
            dma((PARTS, comps)),
            dma((PARTS, comps)),
            dma((2, DEPTH)),
            dma((2, DEPTH)),
            dma((DEPTH, XS)),
            dma((DEPTH, XS)),
        ],
        compiler_params=pltpu.CompilerParams(
            collective_id=0, has_side_effects=True, vmem_limit_bytes=60 << 20
        ),
        name="em_step",
    )(points, means, variances.reshape(1, own), log_weights.reshape(1, own))
    new_means, new_var, new_logw, lik = pl.pallas_call(
        finish,
        out_shape=[
            shape((own, WIDTH), BF16),
            shape((1, own), F32),
            shape((1, own), F32),
            shape((1, npoints), F32),
        ],
        in_specs=[vmem] * 4,
        out_specs=[vmem] * 4,
        name="results",
    )(*results)
    return new_means, new_var.reshape(own), new_logw.reshape(own), lik.reshape(npoints)


def solution(mesh):
    in_specs = (P("dp", None), P(("dp", "comp"), None), P(("dp", "comp")), P(("dp", "comp")))
    out_specs = (P(("dp", "comp"), None), P(("dp", "comp")), P(("dp", "comp")), P("dp"))
    return jax.shard_map(
        per_device, mesh=mesh, in_specs=in_specs, out_specs=out_specs, check_vma=False
    )
```

```python
import functools

import jax
import jax.numpy as jnp
from jax import lax
from jax.experimental import pallas as pl
from jax.experimental.pallas import tpu as pltpu
from jax.sharding import PartitionSpec as P

MESH = pl.DeviceIdType.MESH
F32 = jnp.float32
BF16 = jnp.bfloat16

COMPONENTS = 16384
LOG2E = 1.4426950408889634
LN2 = 0.6931471805599453
TWO_PI = 6.283185307179586

XS, ZS, CORES = 4, 4, 2
Z = 8
DEPTH = 4
WIDTH = 128
OWN = 64
BLOCK = 80
TILE = 512

BASE = {
    (0, 0): 0, (1, 0): 4,
    (0, 1): 8, (1, 1): 12,
    (0, 2): 16, (0, 3): 20,
    (1, 2): 24, (1, 3): 28,
}
CHUNKS = [(1, 2, 3, 5, 6, 7), tuple(range(8, 16)), tuple(range(16, 24)), tuple(range(24, 32)), (0, 4)]
BOUNDS = (0, 4, 8)
PARTS = len(BOUNDS) - 1
NEAR = (0, 1)
FAR = (3, 2)
GROUP = XS * OWN


def split3(v):
    hi = v.astype(BF16).astype(F32)
    mid = (v - hi).astype(BF16).astype(F32)
    lo = (v - hi - mid).astype(BF16).astype(F32)
    return hi, mid, lo


def rows16(parts, lanes):
    row = lax.broadcasted_iota(jnp.int32, (16, lanes), 0)
    out = jnp.zeros((16, lanes), F32)
    for i, part in parts.items():
        out = jnp.where(row == i, jnp.broadcast_to(part, (16, lanes)), out)
    return out


def spread_rows(tile, table):
    return lax.dot_general(tile, table, (((0,), (0,)), ((), ())), preferred_element_type=F32)


def body(
    comps, npoints, total_points,
    points_hbm, means_hbm, var_hbm, logw_hbm,
    out_means, out_var, out_logw, out_lik,
    points, means, var, logw, blocks, centres, scale, pts_t, pts, prob, peak, mass, lse, sums,
    sib_out, sib, sib_stats_out, sib_stats, r_out, r_in,
    p_sem, g_send, g_recv, l_send, l_recv, s_send, s_recv, r_send, r_recv,
):
    dp = lax.axis_index("dp")
    cp = lax.axis_index("comp")
    core = lax.rem(dp, CORES)
    zh = lax.rem(lax.div(dp, CORES), ZS)
    xx = lax.div(dp, CORES * ZS)
    zl = lax.rem(cp, 2)
    yy = lax.div(cp, 2)
    zz = zh * 2 + zl
    sign = 1 - 2 * zl

    def device(dx, dz, dc=0):
        z = lax.rem(zz + dz + Z, Z)
        half = lax.div(z, 2)
        return {
            "dp": lax.rem(xx + dx, XS) * (ZS * CORES) + half * CORES + lax.rem(core + dc, CORES),
            "comp": yy * 2 + z - 2 * half,
        }

    def owner(dx, j, dc=0):
        return device(dx, -sign * j, dc)

    def user(dx, j, dc=0):
        return device(XS - dx, sign * j if j % 2 == 0 else -sign * j, dc)

    sibling = {"dp": dp + 1 - 2 * core}
    c_peer = {d: {"comp": lax.rem(cp + d, comps)} for d in range(1, comps)}
    barrier = pltpu.get_barrier_semaphore()
    everyone = [owner(0, 3), *(c_peer[d] for d in (5, 4, 3, 2, 6, 7, 1))]
    for dx in (2, 1, 3, 0):
        everyone += [owner(dx, 1, dc) for dc in range(CORES)]
    everyone += [owner(0, 2), user(0, 2)]
    everyone += [owner(dx, 0, dc) for dx in (2, 1, 3) for dc in range(CORES)] + [sibling]
    for peer in everyone:
        pl.semaphore_signal(barrier, inc=1, device_id=peer, device_id_type=MESH)
    fetches = [
        pltpu.make_async_copy(src, dst, p_sem.at[i])
        for i, (src, dst) in enumerate(
            [(means_hbm, means), (var_hbm, var), (logw_hbm, logw), (points_hbm, points)]
        )
    ]
    for copy in fetches:
        copy.start()
    for copy in fetches[:3]:
        copy.wait()

    m = means[...]
    mf = m.astype(F32)
    msq = mf * mf
    msq_hi = msq.astype(BF16)
    msq_lo = (msq - msq_hi.astype(F32)).astype(BF16)
    ones = jnp.ones((16, WIDTH), BF16)
    nt = (((1,), (1,)), ((), ()))
    centre_sq = (
        lax.dot_general(ones, msq_hi, nt, preferred_element_type=F32)
        + lax.dot_general(ones, msq_lo, nt, preferred_element_type=F32)
    )[0:1, :]
    v = var[...]
    offset = logw[...] - 0.5 * WIDTH * jnp.log(TWO_PI * v)
    e_hi, e_mid, e_lo = split3(v * offset - 0.5 * centre_sq)
    a_hi, a_mid, a_lo = split3(LOG2E / v)
    blocks[0, 0:OWN, :] = m
    blocks[0, OWN:BLOCK, :] = jnp.zeros((16, WIDTH), BF16)
    blocks[0, OWN:BLOCK, 0:OWN] = rows16(
        {0: e_hi, 1: e_mid, 2: e_lo, 3: a_hi, 4: a_mid, 5: a_lo, 6: jnp.ones_like(v)}, OWN
    ).astype(BF16)

    pts_t[WIDTH + 16 : 2 * WIDTH, :] = jnp.zeros((WIDTH - 16, npoints), BF16)
    row16 = lax.broadcasted_iota(jnp.int32, (16, WIDTH), 0)
    col16 = lax.broadcasted_iota(jnp.int32, (16, WIDTH), 1)
    eye16 = jnp.where(row16 == col16, 1.0, 0.0).astype(BF16)

    def prepare(j, carry):
        for u in range(4):
            at = pl.ds(pl.multiple_of((j * 4 + u) * WIDTH, WIDTH), WIDTH)
            x = points[at, :]
            xt = x.astype(F32).T
            half = -0.5 * jnp.sum(xt * xt, axis=0, keepdims=True)
            b_hi, b_mid, b_lo = split3(half)
            one = jnp.ones_like(half)
            tile = rows16({0: one, 1: one, 2: one, 3: b_hi, 4: b_mid, 5: b_lo}, WIDTH).astype(BF16)
            pts_t[0:WIDTH, at] = xt.astype(BF16)
            pts_t[WIDTH : WIDTH + 16, at] = tile
            pts[at, 0:WIDTH] = x
            pts[at, WIDTH : 2 * WIDTH] = lax.dot_general(
                tile, eye16, (((0,), (0,)), ((), ())), preferred_element_type=F32
            ).astype(BF16)
        return carry

    fetches[3].wait()
    steps = npoints // WIDTH // 4
    lax.fori_loop(0, steps // 4, prepare, 0)

    pl.semaphore_wait(barrier, len(everyone))

    sends = []

    def remote(src, dst, send, recv, peer):
        copy = pltpu.make_async_remote_copy(
            src_ref=src, dst_ref=dst, send_sem=send, recv_sem=recv,
            device_id=peer, device_id_type=MESH,
        )
        copy.start()
        sends.append(copy)

    def arrived(ref, sem):
        pltpu.make_async_copy(ref, ref, sem).wait()

    counter = [0]

    def gather_send(src, dst, n, peer):
        i = counter[0]
        counter[0] += 1
        remote(
            blocks.at[pl.ds(src, n)], blocks.at[pl.ds(dst, n)],
            g_send.at[i], g_recv.at[dst], peer,
        )

    def gather_wait(slot, n):
        arrived(blocks.at[pl.ds(slot, n)], g_recv.at[slot])

    gather_send(0, BASE[1, 0], 1, sibling)
    for j in FAR:
        gather_send(0, BASE[0, j], 1, user(0, j))
    for j in NEAR:
        for dx in (2, 1, 3, 0):
            if (dx, j) != (0, 0):
                for dc in range(CORES):
                    gather_send(0, BASE[dc, j] + dx, 1, user(dx, j, dc))
    lax.fori_loop(steps // 4, steps, prepare, 0)

    row = lax.broadcasted_iota(jnp.int32, (WIDTH, 2 * WIDTH), 0) % 16
    col = lax.broadcasted_iota(jnp.int32, (WIDTH, 2 * WIDTH), 1)
    put = ((row < 3) & (col == row)) | ((row == 6) & (col >= 3) & (col < 6))
    put = put | ((row >= 3) & (row < 6) & (col >= WIDTH))
    table = jnp.where(put, 1.0, 0.0).astype(BF16)

    def expand(c):
        n = len(CHUNKS[c])
        rows = [blocks[s, OWN:BLOCK, :] for s in CHUNKS[c]]
        turned = jnp.concatenate(rows, axis=0).astype(F32).T[0:OWN, :]
        home = lax.broadcasted_iota(jnp.int32, (OWN, 16 * n), 1) // 16
        mine = [jnp.where(home == i, turned, 0.0).astype(BF16) for i in range(n)]
        wide = jnp.dot(
            jnp.concatenate(mine, axis=0), table[0 : 16 * n, :], preferred_element_type=F32
        )
        for i, s in enumerate(CHUNKS[c]):
            at = slice(s * OWN, (s + 1) * OWN)
            centres[at, 0:WIDTH] = blocks[s, 0:OWN, :]
            centres[at, WIDTH : 2 * WIDTH] = wide[i * OWN : (i + 1) * OWN, 0:WIDTH].astype(BF16)
            scale[at, :] = wide[i * OWN : (i + 1) * OWN, WIDTH : 2 * WIDTH]

    def first_pass(c, first, last):
        rows = [slice(b * OWN, (b + 1) * OWN) for b in CHUNKS[c]]
        whole = jnp.concatenate([centres[at, :] for at in rows], axis=0)
        wide = jnp.concatenate([scale[at, :] for at in rows], axis=0)
        wide = jnp.concatenate([wide] * (TILE // WIDTH), axis=1)
        for t in range(first // TILE, last // TILE):
            ns = slice(t * TILE, (t + 1) * TILE)
            y = jnp.dot(whole, pts_t[:, ns], preferred_element_type=F32) * wide
            top = jnp.max(y, axis=0, keepdims=True)
            p = jnp.exp2(y - top)
            for i, at in enumerate(rows):
                prob[at, ns] = p[i * OWN : (i + 1) * OWN, :]
            peak[c : c + 1, ns] = top
            mass[c : c + 1, ns] = jnp.sum(p, axis=0, keepdims=True)

    chunks = len(CHUNKS)
    bounds = [npoints * i // 8 for i in BOUNDS]
    parts = [slice(a, b) for a, b in zip(bounds, bounds[1:])]

    def lse_send(h):
        ns = parts[h]
        top = jnp.max(peak[0:chunks, ns], axis=0, keepdims=True)
        total = jnp.sum(mass[0:chunks, ns] * jnp.exp2(peak[0:chunks, ns] - top), axis=0, keepdims=True)
        n = ns.stop - ns.start
        lse[h, 0, :, 0:n] = top + jnp.log(total) * LOG2E
        for d in range(1, comps):
            remote(
                lse.at[h, 0, :, pl.ds(0, n)], lse.at[h, comps - d, :, pl.ds(0, n)],
                l_send.at[h, d], l_recv.at[h, comps - d], c_peer[d],
            )

    def lse_finish(h):
        ns = parts[h]
        n = ns.stop - ns.start
        for d in range(1, comps):
            arrived(lse.at[h, d, :, pl.ds(0, n)], l_recv.at[h, d])
        got = [lse[h, d, :, 0:n] for d in range(comps)]
        top = functools.reduce(jnp.maximum, got)
        total = sum(jnp.exp2(g - top) for g in got)
        lik = top + jnp.log(total) * LOG2E
        out_lik[:, ns] = lik * LN2
        for c in range(chunks):
            peak[c : c + 1, ns] = jnp.exp2(peak[c : c + 1, ns] - lik)

    gather_wait(BASE[1, 0], 1)
    expand(4)
    first_pass(4, 0, npoints)
    for dc in range(CORES):
        for dx in range(1, XS):
            gather_wait(BASE[dc, 0] + dx, 1)
    expand(0)
    for j in FAR:
        gather_wait(BASE[0, j], 1)
        for d in (2, 1, 3):
            gather_send(BASE[0, j], BASE[0, j] + XS - d, 1, device(d, 0))
    first_pass(0, 0, npoints)
    for dc in range(CORES):
        for dx in range(XS):
            gather_wait(BASE[dc, 1] + dx, 1)
    expand(1)
    first_pass(1, 0, npoints)
    for j in FAR:
        for dx in range(1, XS):
            gather_wait(BASE[0, j] + dx, 1)
        gather_send(BASE[0, j], BASE[1, j], XS, sibling)
    expand(2)
    for h in range(PARTS):
        first_pass(2, parts[h].start, parts[h].stop)
        if h == 0:
            for j in FAR:
                gather_wait(BASE[1, j], XS)
            expand(3)
        first_pass(3, parts[h].start, parts[h].stop)
        lse_send(h)

    def second_pass(h, groups):
        ns = parts[h]
        p = []
        for g in groups:
            for b in range(BASE[g], BASE[g] + XS):
                c = [b in blocks_of for blocks_of in CHUNKS].index(True)
                at = slice(b * OWN, (b + 1) * OWN)
                p.append((prob[at, ns] * peak[c : c + 1, ns]).astype(BF16))
        acc = jnp.dot(jnp.concatenate(p, axis=0), pts[ns, :], preferred_element_type=F32)
        for i, g in enumerate(groups):
            at = slice(BASE[g] * OWN, BASE[g] * OWN + GROUP)
            val = acc[i * GROUP : (i + 1) * GROUP, :]
            val = val if h == 0 else sums[at, :] + val
            sums[at, :] = val
            if h == PARTS - 1 and g[0] == 1:
                sib_out[g[1]] = val[:, 0:WIDTH]
                sib_stats_out[g[1]] = val[:, WIDTH:].T[0:8, :]

    def to_sibling(j):
        remote(sib_out.at[j], sib.at[j], s_send.at[0, j], s_recv.at[0, j], sibling)
        remote(sib_stats_out.at[j], sib_stats.at[j], s_send.at[1, j], s_recv.at[1, j], sibling)

    def pack_stats(cnt, sq):
        c_hi, c_mid, c_lo = split3(cnt)
        s_hi, s_mid, s_lo = split3(sq)
        parts = {0: c_hi, 1: c_mid, 2: c_lo, 3: s_hi, 4: s_mid, 5: s_lo}
        return rows16(parts, cnt.shape[1]).astype(BF16)

    def chip_sum(j):
        at = slice(BASE[0, j] * OWN, BASE[0, j] * OWN + GROUP)
        t = sums[at, WIDTH:].T[0:8, :]
        arrived(sib.at[j], s_recv.at[0, j])
        arrived(sib_stats.at[j], s_recv.at[1, j])
        t = t + sib_stats[j]
        return sums[at, 0:WIDTH] + sib[j], t[0:1, :], t[3:4, :] + t[4:5, :] + t[5:6, :]

    def packet(j, dx, tot, tile):
        r_out[j, dx, 0:OWN, :] = tot.astype(BF16)
        r_out[j, dx, OWN:BLOCK, :] = tile

    def send_packet(j, dx, slot, peer):
        remote(r_out.at[j, dx], r_in.at[j, slot], r_send.at[j, dx], r_recv.at[j, slot], peer)

    def to_owner(j):
        tot, cnt, sq = chip_sum(j)
        tile = pack_stats(cnt, sq)
        for dx in (2, 1, 3, 0):
            if dx == 0 and (j == 0 or j in FAR):
                continue
            lanes = slice((dx // 2) * WIDTH, (dx // 2 + 1) * WIDTH)
            packet(j, dx, tot[dx * OWN : (dx + 1) * OWN, :], tile[:, lanes])
            if j in FAR:
                send_packet(j, dx, XS - dx, device(dx, 0))
            else:
                send_packet(j, dx, dx, owner(dx, j))
        return tot[0:OWN, :], cnt[:, 0:WIDTH], sq[:, 0:WIDTH]

    def rows_of(tile):
        t = tile.astype(F32)
        return t[0:1, :] + t[1:2, :] + t[2:3, :], t[3:4, :] + t[4:5, :] + t[5:6, :]

    def add_packets(total, even, odd, slots):
        even, odd = list(even), [jnp.zeros_like(e) if odd is None else o for e, o in zip(even, odd or even)]
        for j, dx in slots:
            arrived(r_in.at[j, dx], r_recv.at[j, dx])
            total = total + r_in[j, dx, 0:OWN, :].astype(F32)
            got = rows_of(r_in[j, dx, OWN:BLOCK, :])
            if dx % 2 == 0:
                even = [a + b for a, b in zip(even, got)]
            if dx % 2 == 1 or (dx == 0 and j in FAR):
                odd = [a + b for a, b in zip(odd, got)]
        return total, even, odd

    steps = [[(1, 3), (1, 2)], [(0, 3), (0, 2)], [(1, 1), (1, 0)], [(0, 1), (0, 0)]]
    for h in range(PARTS - 1):
        lse_finish(h)
        for step in steps:
            second_pass(h, step)
    lse_finish(PARTS - 1)
    second_pass(PARTS - 1, steps[0])
    to_sibling(3)
    to_sibling(2)
    second_pass(PARTS - 1, steps[1])
    partial = {j: to_owner(j) for j in FAR}
    second_pass(PARTS - 1, steps[2])
    to_sibling(1)
    to_sibling(0)
    second_pass(PARTS - 1, steps[3])
    to_owner(1)
    own_total, *own_even = to_owner(0)
    lane = lax.broadcasted_iota(jnp.int32, (1, WIDTH), 1)
    for j in FAR:
        total, *even = partial[j]
        total, even, odd = add_packets(total, even, None, [(j, dx) for dx in range(1, XS)])
        packet(j, 0, total, pack_stats(*[jnp.where(lane < OWN, a, b) for a, b in zip(even, odd)]))
        send_packet(j, 0, 0, owner(0, j))
    slots = [(j, dx) for j in NEAR for dx in range(XS) if (dx, j) != (0, 0)]
    total, even, odd = add_packets(own_total, own_even, None, slots + [(j, 0) for j in FAR])
    row, col = row[0:16, :], col[0:16, :]
    is_cnt = (row < 3) & (col < WIDTH)
    is_sq = (row >= 3) & (row < 6) & (col >= WIDTH)
    columns = jnp.where(is_cnt | is_sq, 1.0, 0.0).astype(BF16)
    stats = 0.0
    for i, rows in enumerate((even, odd)):
        wide = spread_rows(pack_stats(*rows), columns)
        stats = stats + wide[i * OWN : (i + 1) * OWN, :]

    counts = stats[:, 0:WIDTH]
    squares = -2.0 * stats[:, WIDTH:]
    prior = means[...].astype(F32)
    prior_var = LOG2E / scale[0:OWN, :]
    denom = counts + 1.0
    centre = (total + prior) / denom
    cross = jnp.sum(centre * total, axis=1, keepdims=True)
    own_sq = jnp.sum(centre * centre, axis=1, keepdims=True)
    spread = (squares - 2.0 * cross + counts * own_sq + WIDTH * prior_var) / (WIDTH * denom)
    weight = jnp.log(denom / (total_points + COMPONENTS))
    out_means[...] = centre.astype(BF16)
    lane = lax.broadcasted_iota(jnp.int32, (OWN, WIDTH), 1)
    flat = jnp.where(lane == 0, spread, weight).T
    out_var[...] = flat[0:1, :]
    out_logw[...] = flat[1:2, :]

    for copy in sends:
        copy.wait_send()


def finish(*refs):
    for src, dst in zip(refs[:4], refs[4:]):
        dst[...] = src[...]


def per_device(points, means, variances, log_weights):
    comps = lax.axis_size("comp")
    npoints = points.shape[0]
    own = means.shape[0]
    group = own * lax.axis_size("dp")
    vmem = pl.BlockSpec(memory_space=pltpu.VMEM)
    shape = jax.ShapeDtypeStruct
    dma = pltpu.SemaphoreType.DMA
    results = pl.pallas_call(
        functools.partial(body, comps, npoints, npoints * lax.axis_size("dp")),
        out_shape=[
            shape((own, WIDTH), BF16),
            shape((1, own), F32),
            shape((1, own), F32),
            shape((1, npoints), F32),
        ],
        in_specs=[pl.BlockSpec(memory_space=pl.ANY)] * 4,
        out_specs=[vmem] * 4,
        scratch_shapes=[
            pltpu.VMEM((npoints, WIDTH), BF16),
            pltpu.VMEM((own, WIDTH), BF16),
            pltpu.VMEM((1, own), F32),
            pltpu.VMEM((1, own), F32),
            pltpu.VMEM((32, BLOCK, WIDTH), BF16),
            pltpu.VMEM((group, 2 * WIDTH), BF16),
            pltpu.VMEM((group, WIDTH), F32),
            pltpu.VMEM((2 * WIDTH, npoints), BF16),
            pltpu.VMEM((npoints, 2 * WIDTH), BF16),
            pltpu.VMEM((group, npoints), F32),
            pltpu.VMEM((8, npoints), F32),
            pltpu.VMEM((8, npoints), F32),
            pltpu.VMEM((PARTS, comps, 1, npoints // 2), F32),
            pltpu.VMEM((group, 2 * WIDTH), F32),
            pltpu.VMEM((DEPTH, GROUP, WIDTH), F32),
            pltpu.VMEM((DEPTH, GROUP, WIDTH), F32),
            pltpu.VMEM((DEPTH, 8, GROUP), F32),
            pltpu.VMEM((DEPTH, 8, GROUP), F32),
            pltpu.VMEM((DEPTH, XS, BLOCK, WIDTH), BF16),
            pltpu.VMEM((DEPTH, XS, BLOCK, WIDTH), BF16),
            dma((4,)),
            dma((32,)),
            dma((32,)),
            dma((PARTS, comps)),
            dma((PARTS, comps)),
            dma((2, DEPTH)),
            dma((2, DEPTH)),
            dma((DEPTH, XS)),
            dma((DEPTH, XS)),
        ],
        compiler_params=pltpu.CompilerParams(
            collective_id=0, has_side_effects=True, vmem_limit_bytes=60 << 20
        ),
        name="em_step",
    )(points, means, variances.reshape(1, own), log_weights.reshape(1, own))
    new_means, new_var, new_logw, lik = pl.pallas_call(
        finish,
        out_shape=[
            shape((own, WIDTH), BF16),
            shape((1, own), F32),
            shape((1, own), F32),
            shape((1, npoints), F32),
        ],
        in_specs=[vmem] * 4,
        out_specs=[vmem] * 4,
        name="results",
    )(*results)
    return new_means, new_var.reshape(own), new_logw.reshape(own), lik.reshape(npoints)


def solution(mesh):
    in_specs = (P("dp", None), P(("dp", "comp"), None), P(("dp", "comp")), P(("dp", "comp")))
    out_specs = (P(("dp", "comp"), None), P(("dp", "comp")), P(("dp", "comp")), P("dp"))
    return jax.shard_map(
        per_device, mesh=mesh, in_specs=in_specs, out_specs=out_specs, check_vma=False
    )
```

```python
import functools

import jax
import jax.numpy as jnp
from jax import lax
from jax.experimental import pallas as pl
from jax.experimental.pallas import tpu as pltpu
from jax.sharding import PartitionSpec as P

MESH = pl.DeviceIdType.MESH
F32 = jnp.float32
BF16 = jnp.bfloat16

COMPONENTS = 16384
LOG2E = 1.4426950408889634
LN2 = 0.6931471805599453
TWO_PI = 6.283185307179586

XS, ZS, CORES = 4, 4, 2
Z = 8
DEPTH = 4
WIDTH = 128
OWN = 64
BLOCK = 80
TILE = 512

BASE = {
    (0, 0): 0, (1, 0): 4,
    (0, 1): 8, (1, 1): 12,
    (0, 2): 16, (0, 3): 20,
    (1, 2): 24, (1, 3): 28,
}
CHUNKS = [(1, 2, 3, 5, 6, 7), tuple(range(8, 16)), tuple(range(16, 24)), tuple(range(24, 32)), (0, 4)]
BOUNDS = (0, 4, 8)
PARTS = len(BOUNDS) - 1
NEAR = (0, 1)
FAR = (3, 2)
GROUP = XS * OWN


def split3(v):
    hi = v.astype(BF16).astype(F32)
    mid = (v - hi).astype(BF16).astype(F32)
    lo = (v - hi - mid).astype(BF16).astype(F32)
    return hi, mid, lo


def rows16(parts, lanes):
    row = lax.broadcasted_iota(jnp.int32, (16, lanes), 0)
    out = jnp.zeros((16, lanes), F32)
    for i, part in parts.items():
        out = jnp.where(row == i, jnp.broadcast_to(part, (16, lanes)), out)
    return out


def spread_rows(tile, table):
    return lax.dot_general(tile, table, (((0,), (0,)), ((), ())), preferred_element_type=F32)


def body(
    comps, npoints, total_points,
    points_hbm, means_hbm, var_hbm, logw_hbm,
    out_means, out_var, out_logw, out_lik,
    points, means, var, logw, blocks, centres, scale, pts_t, pts, prob, peak, mass, lse, sums,
    sib_out, sib, sib_stats_out, sib_stats, r_out, r_in,
    p_sem, g_send, g_recv, l_send, l_recv, s_send, s_recv, r_send, r_recv,
):
    dp = lax.axis_index("dp")
    cp = lax.axis_index("comp")
    core = lax.rem(dp, CORES)
    zh = lax.rem(lax.div(dp, CORES), ZS)
    xx = lax.div(dp, CORES * ZS)
    zl = lax.rem(cp, 2)
    yy = lax.div(cp, 2)
    zz = zh * 2 + zl
    sign = 1 - 2 * zl

    def device(dx, dz, dc=0):
        z = lax.rem(zz + dz + Z, Z)
        half = lax.div(z, 2)
        return {
            "dp": lax.rem(xx + dx, XS) * (ZS * CORES) + half * CORES + lax.rem(core + dc, CORES),
            "comp": yy * 2 + z - 2 * half,
        }

    def owner(dx, j, dc=0):
        return device(dx, -sign * j, dc)

    def user(dx, j, dc=0):
        return device(XS - dx, sign * j if j % 2 == 0 else -sign * j, dc)

    sibling = {"dp": dp + 1 - 2 * core}
    c_peer = {d: {"comp": lax.rem(cp + d, comps)} for d in range(1, comps)}
    barrier = pltpu.get_barrier_semaphore()
    everyone = [owner(0, 3), *(c_peer[d] for d in (5, 4, 3, 2, 6, 7, 1))]
    for dx in (2, 1, 3, 0):
        everyone += [owner(dx, 1, dc) for dc in range(CORES)]
    everyone += [owner(0, 2), user(0, 2)]
    everyone += [owner(dx, 0, dc) for dx in (2, 1, 3) for dc in range(CORES)] + [sibling]
    for peer in everyone:
        pl.semaphore_signal(barrier, inc=1, device_id=peer, device_id_type=MESH)
    fetches = [
        pltpu.make_async_copy(src, dst, p_sem.at[i])
        for i, (src, dst) in enumerate(
            [(means_hbm, means), (var_hbm, var), (logw_hbm, logw), (points_hbm, points)]
        )
    ]
    for copy in fetches:
        copy.start()
    for copy in fetches[:3]:
        copy.wait()

    m = means[...]
    mf = m.astype(F32)
    msq = mf * mf
    msq_hi = msq.astype(BF16)
    msq_lo = (msq - msq_hi.astype(F32)).astype(BF16)
    ones = jnp.ones((16, WIDTH), BF16)
    nt = (((1,), (1,)), ((), ()))
    centre_sq = (
        lax.dot_general(ones, msq_hi, nt, preferred_element_type=F32)
        + lax.dot_general(ones, msq_lo, nt, preferred_element_type=F32)
    )[0:1, :]
    v = var[...]
    offset = logw[...] - 0.5 * WIDTH * jnp.log(TWO_PI * v)
    e_hi, e_mid, e_lo = split3(v * offset - 0.5 * centre_sq)
    a_hi, a_mid, a_lo = split3(LOG2E / v)
    blocks[0, 0:OWN, :] = m
    blocks[0, OWN:BLOCK, :] = jnp.zeros((16, WIDTH), BF16)
    blocks[0, OWN:BLOCK, 0:OWN] = rows16(
        {0: e_hi, 1: e_mid, 2: e_lo, 3: a_hi, 4: a_mid, 5: a_lo, 6: jnp.ones_like(v)}, OWN
    ).astype(BF16)

    pts_t[WIDTH + 16 : 2 * WIDTH, :] = jnp.zeros((WIDTH - 16, npoints), BF16)
    row16 = lax.broadcasted_iota(jnp.int32, (16, WIDTH), 0)
    col16 = lax.broadcasted_iota(jnp.int32, (16, WIDTH), 1)
    eye16 = jnp.where(row16 == col16, 1.0, 0.0).astype(BF16)

    def prepare(j, carry):
        for u in range(4):
            at = pl.ds(pl.multiple_of((j * 4 + u) * WIDTH, WIDTH), WIDTH)
            x = points[at, :]
            xt = x.astype(F32).T
            half = -0.5 * jnp.sum(xt * xt, axis=0, keepdims=True)
            b_hi, b_mid, b_lo = split3(half)
            one = jnp.ones_like(half)
            tile = rows16({0: one, 1: one, 2: one, 3: b_hi, 4: b_mid, 5: b_lo}, WIDTH).astype(BF16)
            pts_t[0:WIDTH, at] = xt.astype(BF16)
            pts_t[WIDTH : WIDTH + 16, at] = tile
            pts[at, 0:WIDTH] = x
            pts[at, WIDTH : 2 * WIDTH] = lax.dot_general(
                tile, eye16, (((0,), (0,)), ((), ())), preferred_element_type=F32
            ).astype(BF16)
        return carry

    fetches[3].wait()
    steps = npoints // WIDTH // 4
    lax.fori_loop(0, steps // 4, prepare, 0)

    pl.semaphore_wait(barrier, len(everyone))

    sends = []

    def remote(src, dst, send, recv, peer):
        copy = pltpu.make_async_remote_copy(
            src_ref=src, dst_ref=dst, send_sem=send, recv_sem=recv,
            device_id=peer, device_id_type=MESH,
        )
        copy.start()
        sends.append(copy)

    def arrived(ref, sem):
        pltpu.make_async_copy(ref, ref, sem).wait()

    counter = [0]

    def gather_send(src, dst, n, peer):
        i = counter[0]
        counter[0] += 1
        remote(
            blocks.at[pl.ds(src, n)], blocks.at[pl.ds(dst, n)],
            g_send.at[i], g_recv.at[dst], peer,
        )

    def gather_wait(slot, n):
        arrived(blocks.at[pl.ds(slot, n)], g_recv.at[slot])

    gather_send(0, BASE[1, 0], 1, sibling)
    for j in FAR:
        gather_send(0, BASE[0, j], 1, user(0, j))
    for j in NEAR:
        for dx in (2, 1, 3, 0):
            if (dx, j) != (0, 0):
                for dc in range(CORES):
                    gather_send(0, BASE[dc, j] + dx, 1, user(dx, j, dc))
    lax.fori_loop(steps // 4, steps, prepare, 0)

    row = lax.broadcasted_iota(jnp.int32, (WIDTH, 2 * WIDTH), 0) % 16
    col = lax.broadcasted_iota(jnp.int32, (WIDTH, 2 * WIDTH), 1)
    put = ((row < 3) & (col == row)) | ((row == 6) & (col >= 3) & (col < 6))
    put = put | ((row >= 3) & (row < 6) & (col >= WIDTH))
    table = jnp.where(put, 1.0, 0.0).astype(BF16)

    def expand(c):
        n = len(CHUNKS[c])
        rows = [blocks[s, OWN:BLOCK, :] for s in CHUNKS[c]]
        turned = jnp.concatenate(rows, axis=0).astype(F32).T[0:OWN, :]
        home = lax.broadcasted_iota(jnp.int32, (OWN, 16 * n), 1) // 16
        mine = [jnp.where(home == i, turned, 0.0).astype(BF16) for i in range(n)]
        wide = jnp.dot(
            jnp.concatenate(mine, axis=0), table[0 : 16 * n, :], preferred_element_type=F32
        )
        for i, s in enumerate(CHUNKS[c]):
            at = slice(s * OWN, (s + 1) * OWN)
            centres[at, 0:WIDTH] = blocks[s, 0:OWN, :]
            centres[at, WIDTH : 2 * WIDTH] = wide[i * OWN : (i + 1) * OWN, 0:WIDTH].astype(BF16)
            scale[at, :] = wide[i * OWN : (i + 1) * OWN, WIDTH : 2 * WIDTH]

    def first_pass(c, first, last):
        rows = [slice(b * OWN, (b + 1) * OWN) for b in CHUNKS[c]]
        whole = jnp.concatenate([centres[at, :] for at in rows], axis=0)
        wide = jnp.concatenate([scale[at, :] for at in rows], axis=0)
        wide = jnp.concatenate([wide] * (TILE // WIDTH), axis=1)
        for t in range(first // TILE, last // TILE):
            ns = slice(t * TILE, (t + 1) * TILE)
            y = jnp.dot(whole, pts_t[:, ns], preferred_element_type=F32) * wide
            top = jnp.max(y, axis=0, keepdims=True)
            p = jnp.exp2(y - top)
            for i, at in enumerate(rows):
                prob[at, ns] = p[i * OWN : (i + 1) * OWN, :]
            peak[c : c + 1, ns] = top
            mass[c : c + 1, ns] = jnp.sum(p, axis=0, keepdims=True)

    chunks = len(CHUNKS)
    bounds = [npoints * i // 8 for i in BOUNDS]
    parts = [slice(a, b) for a, b in zip(bounds, bounds[1:])]

    def lse_send(h):
        ns = parts[h]
        top = jnp.max(peak[0:chunks, ns], axis=0, keepdims=True)
        total = jnp.sum(mass[0:chunks, ns] * jnp.exp2(peak[0:chunks, ns] - top), axis=0, keepdims=True)
        n = ns.stop - ns.start
        lse[h, 0, :, 0:n] = top + jnp.log(total) * LOG2E
        for d in range(1, comps):
            remote(
                lse.at[h, 0, :, pl.ds(0, n)], lse.at[h, comps - d, :, pl.ds(0, n)],
                l_send.at[h, d], l_recv.at[h, comps - d], c_peer[d],
            )

    def lse_finish(h):
        ns = parts[h]
        n = ns.stop - ns.start
        for d in range(1, comps):
            arrived(lse.at[h, d, :, pl.ds(0, n)], l_recv.at[h, d])
        got = [lse[h, d, :, 0:n] for d in range(comps)]
        top = functools.reduce(jnp.maximum, got)
        total = sum(jnp.exp2(g - top) for g in got)
        lik = top + jnp.log(total) * LOG2E
        out_lik[:, ns] = lik * LN2
        for c in range(chunks):
            peak[c : c + 1, ns] = jnp.exp2(peak[c : c + 1, ns] - lik)

    gather_wait(BASE[1, 0], 1)
    expand(4)
    first_pass(4, 0, npoints)
    for dc in range(CORES):
        for dx in range(1, XS):
            gather_wait(BASE[dc, 0] + dx, 1)
    expand(0)
    for j in FAR:
        gather_wait(BASE[0, j], 1)
        for d in (2, 1, 3):
            gather_send(BASE[0, j], BASE[0, j] + XS - d, 1, device(d, 0))
    first_pass(0, 0, npoints)
    for dc in range(CORES):
        for dx in range(XS):
            gather_wait(BASE[dc, 1] + dx, 1)
    expand(1)
    first_pass(1, 0, npoints)
    for j in FAR:
        for dx in range(1, XS):
            gather_wait(BASE[0, j] + dx, 1)
        gather_send(BASE[0, j], BASE[1, j], XS, sibling)
    expand(2)
    for h in range(PARTS):
        first_pass(2, parts[h].start, parts[h].stop)
        if h == 0:
            for j in FAR:
                gather_wait(BASE[1, j], XS)
            expand(3)
        first_pass(3, parts[h].start, parts[h].stop)
        lse_send(h)

    def second_pass(h, groups):
        ns = parts[h]
        p = []
        for g in groups:
            for b in range(BASE[g], BASE[g] + XS):
                c = [b in blocks_of for blocks_of in CHUNKS].index(True)
                at = slice(b * OWN, (b + 1) * OWN)
                p.append((prob[at, ns] * peak[c : c + 1, ns]).astype(BF16))
        acc = jnp.dot(jnp.concatenate(p, axis=0), pts[ns, :], preferred_element_type=F32)
        for i, g in enumerate(groups):
            at = slice(BASE[g] * OWN, BASE[g] * OWN + GROUP)
            val = acc[i * GROUP : (i + 1) * GROUP, :]
            val = val if h == 0 else sums[at, :] + val
            sums[at, :] = val
            if h == PARTS - 1 and g[0] == 1:
                sib_out[g[1]] = val[:, 0:WIDTH]
                sib_stats_out[g[1]] = val[:, WIDTH:].T[0:8, :]

    def to_sibling(j):
        remote(sib_out.at[j], sib.at[j], s_send.at[0, j], s_recv.at[0, j], sibling)
        remote(sib_stats_out.at[j], sib_stats.at[j], s_send.at[1, j], s_recv.at[1, j], sibling)

    def pack_stats(cnt, sq):
        c_hi, c_mid, c_lo = split3(cnt)
        s_hi, s_mid, s_lo = split3(sq)
        parts = {0: c_hi, 1: c_mid, 2: c_lo, 3: s_hi, 4: s_mid, 5: s_lo}
        return rows16(parts, cnt.shape[1]).astype(BF16)

    def chip_sum(j):
        at = slice(BASE[0, j] * OWN, BASE[0, j] * OWN + GROUP)
        t = sums[at, WIDTH:].T[0:8, :]
        arrived(sib.at[j], s_recv.at[0, j])
        arrived(sib_stats.at[j], s_recv.at[1, j])
        t = t + sib_stats[j]
        return sums[at, 0:WIDTH] + sib[j], t[0:1, :], t[3:4, :] + t[4:5, :] + t[5:6, :]

    def packet(j, dx, tot, tile):
        r_out[j, dx, 0:OWN, :] = tot.astype(BF16)
        r_out[j, dx, OWN:BLOCK, :] = tile

    def send_packet(j, dx, slot, peer):
        remote(r_out.at[j, dx], r_in.at[j, slot], r_send.at[j, dx], r_recv.at[j, slot], peer)

    def to_owner(j):
        tot, cnt, sq = chip_sum(j)
        tile = pack_stats(cnt, sq)
        for dx in (2, 1, 3, 0):
            if dx == 0 and (j == 0 or j in FAR):
                continue
            lanes = slice((dx // 2) * WIDTH, (dx // 2 + 1) * WIDTH)
            packet(j, dx, tot[dx * OWN : (dx + 1) * OWN, :], tile[:, lanes])
            if j in FAR:
                send_packet(j, dx, XS - dx, device(dx, 0))
            else:
                send_packet(j, dx, dx, owner(dx, j))
        return tot[0:OWN, :], cnt[:, 0:WIDTH], sq[:, 0:WIDTH]

    def rows_of(tile):
        t = tile.astype(F32)
        return t[0:1, :] + t[1:2, :] + t[2:3, :], t[3:4, :] + t[4:5, :] + t[5:6, :]

    def add_packets(total, even, odd, slots):
        even, odd = list(even), [jnp.zeros_like(e) if odd is None else o for e, o in zip(even, odd or even)]
        for j, dx in slots:
            arrived(r_in.at[j, dx], r_recv.at[j, dx])
            total = total + r_in[j, dx, 0:OWN, :].astype(F32)
            got = rows_of(r_in[j, dx, OWN:BLOCK, :])
            if dx % 2 == 0:
                even = [a + b for a, b in zip(even, got)]
            if dx % 2 == 1 or (dx == 0 and j in FAR):
                odd = [a + b for a, b in zip(odd, got)]
        return total, even, odd

    steps = [[(1, 3), (1, 2)], [(0, 3), (0, 2)], [(1, 1), (1, 0)], [(0, 1), (0, 0)]]
    for h in range(PARTS - 1):
        lse_finish(h)
        for step in steps:
            second_pass(h, step)
    lse_finish(PARTS - 1)
    for j in FAR:
        second_pass(PARTS - 1, [(1, j)])
        to_sibling(j)
    second_pass(PARTS - 1, steps[1])
    partial = {j: to_owner(j) for j in FAR}
    second_pass(PARTS - 1, steps[2])
    to_sibling(1)
    to_sibling(0)
    second_pass(PARTS - 1, steps[3])
    to_owner(1)
    own_total, *own_even = to_owner(0)
    lane = lax.broadcasted_iota(jnp.int32, (1, WIDTH), 1)
    for j in FAR:
        total, *even = partial[j]
        total, even, odd = add_packets(total, even, None, [(j, dx) for dx in range(1, XS)])
        packet(j, 0, total, pack_stats(*[jnp.where(lane < OWN, a, b) for a, b in zip(even, odd)]))
        send_packet(j, 0, 0, owner(0, j))
    slots = [(j, dx) for j in NEAR for dx in range(XS) if (dx, j) != (0, 0)]
    total, even, odd = add_packets(own_total, own_even, None, slots + [(j, 0) for j in FAR])
    row, col = row[0:16, :], col[0:16, :]
    is_cnt = (row < 3) & (col < WIDTH)
    is_sq = (row >= 3) & (row < 6) & (col >= WIDTH)
    columns = jnp.where(is_cnt | is_sq, 1.0, 0.0).astype(BF16)
    stats = 0.0
    for i, rows in enumerate((even, odd)):
        wide = spread_rows(pack_stats(*rows), columns)
        stats = stats + wide[i * OWN : (i + 1) * OWN, :]

    counts = stats[:, 0:WIDTH]
    squares = -2.0 * stats[:, WIDTH:]
    prior = means[...].astype(F32)
    prior_var = LOG2E / scale[0:OWN, :]
    denom = counts + 1.0
    centre = (total + prior) / denom
    cross = jnp.sum(centre * total, axis=1, keepdims=True)
    own_sq = jnp.sum(centre * centre, axis=1, keepdims=True)
    spread = (squares - 2.0 * cross + counts * own_sq + WIDTH * prior_var) / (WIDTH * denom)
    weight = jnp.log(denom / (total_points + COMPONENTS))
    out_means[...] = centre.astype(BF16)
    lane = lax.broadcasted_iota(jnp.int32, (OWN, WIDTH), 1)
    flat = jnp.where(lane == 0, spread, weight).T
    out_var[...] = flat[0:1, :]
    out_logw[...] = flat[1:2, :]

    for copy in sends:
        copy.wait_send()


def finish(*refs):
    for src, dst in zip(refs[:4], refs[4:]):
        dst[...] = src[...]


def per_device(points, means, variances, log_weights):
    comps = lax.axis_size("comp")
    npoints = points.shape[0]
    own = means.shape[0]
    group = own * lax.axis_size("dp")
    vmem = pl.BlockSpec(memory_space=pltpu.VMEM)
    shape = jax.ShapeDtypeStruct
    dma = pltpu.SemaphoreType.DMA
    results = pl.pallas_call(
        functools.partial(body, comps, npoints, npoints * lax.axis_size("dp")),
        out_shape=[
            shape((own, WIDTH), BF16),
            shape((1, own), F32),
            shape((1, own), F32),
            shape((1, npoints), F32),
        ],
        in_specs=[pl.BlockSpec(memory_space=pl.ANY)] * 4,
        out_specs=[vmem] * 4,
        scratch_shapes=[
            pltpu.VMEM((npoints, WIDTH), BF16),
            pltpu.VMEM((own, WIDTH), BF16),
            pltpu.VMEM((1, own), F32),
            pltpu.VMEM((1, own), F32),
            pltpu.VMEM((32, BLOCK, WIDTH), BF16),
            pltpu.VMEM((group, 2 * WIDTH), BF16),
            pltpu.VMEM((group, WIDTH), F32),
            pltpu.VMEM((2 * WIDTH, npoints), BF16),
            pltpu.VMEM((npoints, 2 * WIDTH), BF16),
            pltpu.VMEM((group, npoints), F32),
            pltpu.VMEM((8, npoints), F32),
            pltpu.VMEM((8, npoints), F32),
            pltpu.VMEM((PARTS, comps, 1, npoints // 2), F32),
            pltpu.VMEM((group, 2 * WIDTH), F32),
            pltpu.VMEM((DEPTH, GROUP, WIDTH), F32),
            pltpu.VMEM((DEPTH, GROUP, WIDTH), F32),
            pltpu.VMEM((DEPTH, 8, GROUP), F32),
            pltpu.VMEM((DEPTH, 8, GROUP), F32),
            pltpu.VMEM((DEPTH, XS, BLOCK, WIDTH), BF16),
            pltpu.VMEM((DEPTH, XS, BLOCK, WIDTH), BF16),
            dma((4,)),
            dma((32,)),
            dma((32,)),
            dma((PARTS, comps)),
            dma((PARTS, comps)),
            dma((2, DEPTH)),
            dma((2, DEPTH)),
            dma((DEPTH, XS)),
            dma((DEPTH, XS)),
        ],
        compiler_params=pltpu.CompilerParams(
            collective_id=0, has_side_effects=True, vmem_limit_bytes=60 << 20
        ),
        name="em_step",
    )(points, means, variances.reshape(1, own), log_weights.reshape(1, own))
    new_means, new_var, new_logw, lik = pl.pallas_call(
        finish,
        out_shape=[
            shape((own, WIDTH), BF16),
            shape((1, own), F32),
            shape((1, own), F32),
            shape((1, npoints), F32),
        ],
        in_specs=[vmem] * 4,
        out_specs=[vmem] * 4,
        name="results",
    )(*results)
    return new_means, new_var.reshape(own), new_logw.reshape(own), lik.reshape(npoints)


def solution(mesh):
    in_specs = (P("dp", None), P(("dp", "comp"), None), P(("dp", "comp")), P(("dp", "comp")))
    out_specs = (P(("dp", "comp"), None), P(("dp", "comp")), P(("dp", "comp")), P("dp"))
    return jax.shard_map(
        per_device, mesh=mesh, in_specs=in_specs, out_specs=out_specs, check_vma=False
    )
```
